32 devices in a mesh: grp: 2 (over x), ax: 8 (over z, y), nr: 2 (over core).
Axes of the slice: x: 2, y: 2, z: 4, core: 2. Of those that a mesh axis runs over, the one named last changes fastest.
Arguments:
- pair_map: bfloat16 [1024, 512, 128], P(('grp', 'ax', 'nr')), parts along dimension 0, may hold values from -24 to 24
- chain_ids: int32 [1024], P('grp'), parts along dimension 0, may hold values from 0 to 7, never falling along the last dimension, each value on 1 to 128 neighbouring positions
- token_mask: int32 [1024], P('grp'), parts along dimension 0, may hold values 0 or 1
- band_start: int32 [2], P('grp'), parts along dimension 0, may hold values from 0 to 464
- chain_embed: float32 [128], replicated, may hold values from -8 to 8
- gain_in: float32 [128], replicated, may hold values from 0.1 to 1.9
- gain_out: float32 [128], replicated, may hold values from 0.1 to 1.9
- w_left: bfloat16 [128, 256], P(None, 'nr'), may hold values from -0.5 to 0.5
- w_right: bfloat16 [128, 256], P(None, 'nr'), may hold values from -0.5 to 0.5
- w_gate: bfloat16 [128, 128], P(None, 'nr'), may hold values from -0.5 to 0.5
- w_out: bfloat16 [128, 128], P(None, 'nr'), may hold values from -0.5 to 0.5
Outputs:
- update: bfloat16 [1024, 48, 128], P(('grp', 'ax', 'nr')), parts along dimension 0
The draws below stay inside these ranges and needn't reach their ends.
There are 2 independent parts, one for each index of `grp`. The reference program is written for one: setup_inputs(seed, part) draws one part's arguments, and reference() takes and returns one part's arrays. A program takes and returns all parts, laid end to end along the dimension named above; an argument that names none is the same for every part. Nothing has to cross between parts.
Inputs may be any that keep to these rules, and one draw needn't show every extreme that they name: `chain_ids`: non-decreasing along tokens; a chain holds 1 to 128 tokens, one exactly 128.
All inputs are finite; a program needn't handle non-finite values.
Results may differ from the reference program's by a relative error of at most 0.0075.
Values may be sent and summed in bfloat16 or wider, within the bound.
No kernel may reach another device: no remote copies, remote signals or barrier semaphores. Data moves between devices by JAX's collectives and lax.ppermute only.
A program may use at most 192 MiB of HBM per device.

```python
import math
import jax
import jax.numpy as jnp
import numpy as np
from jax import lax

C = 128
ROWS_DEV = 32
BAND = 48
CHAINS = 8
N = 512


def draw_pair_map(key, part):
    key = jax.random.fold_in(key, 11)
    key_channel, key_cell, key_base = jax.random.split(key, 3)
    channel_scale = jnp.exp(jax.random.uniform(key_channel, (C,), jnp.float32, 0.0, math.log(10.0)))
    cell_scale = jnp.exp(jax.random.uniform(key_cell, (N, N, 1), jnp.float32, 0.0, math.log(4.0)))
    base_values = jax.random.truncated_normal(key_base, -6.0, 6.0, (N, N, C), jnp.float32)
    return (0.1 * base_values * channel_scale * cell_scale).astype(jnp.bfloat16)


def touch_ends(entries, key, smallest, high):
    longest = entries.shape.index(max(entries.shape))
    spots = []
    for shift in (0, 1):
        where = [jax.random.randint(jax.random.fold_in(key, axis), (), 0, length) for axis, length in enumerate(entries.shape)]
        where[longest] = (where[longest] + shift) % entries.shape[longest]
        spots.append(tuple(where))
    return entries.at[spots[0]].set(smallest).at[spots[1]].set(high)


def steps_of(own_key, dims, cuts, least, largest):
    def one(dim, parts):
        heights = jax.random.uniform(jax.random.fold_in(jax.random.fold_in(own_key, 6), dim), (parts,), jnp.float32, least / len(cuts), largest / len(cuts))
        return jnp.repeat(jnp.exp(heights), dims[dim] // parts).reshape((-1,) + (1,) * (len(dims) - dim - 1))

    gain = one(*cuts[0])
    for cut in cuts[1:]:
        gain = gain * one(*cut)
    return gain


def profile(number_of, total, limit, lean):
    weights = [(1 << 20) // math.isqrt(rank ** lean) + 1 for rank in range(2, number_of + 1)]
    rest, counts = total - limit - (number_of - 1), [1] * (number_of - 1)
    while rest > 0:
        free = [i for i in range(number_of - 1) if counts[i] < limit]
        mass, left = sum([weights[i] for i in free]), rest
        for i in free:
            more = min(limit - counts[i], max(1, left * weights[i] // mass), rest)
            counts[i] = counts[i] + more
            rest = rest - more
    return np.array([limit] + counts)


def uneven_parts(own_key, count, total, limit, lean):
    if count == 2:
        one = jax.random.randint(own_key, (), max(1, total - limit), min(limit, total - 1) + 1)
        return jnp.stack([one, total - one])
    tallies = jnp.asarray(profile(count, total, limit, lean), jnp.int32)
    couples = (count - 1) // 2
    donor, taker = tallies[1:1 + 2 * couples:2], tallies[2:2 + 2 * couples:2]
    margin = jnp.minimum(donor - 1, limit - taker)
    moved = jax.random.randint(jax.random.fold_in(own_key, 1), (couples,), 0, 1 << 20) % (margin + 1)
    tallies = tallies.at[1:1 + 2 * couples:2].set(donor - moved).at[2:2 + 2 * couples:2].set(taker + moved)
    return tallies[jax.random.permutation(jax.random.fold_in(own_key, 2), count)]


def bell_draw(stream_key, extent, deviation, limit, cuts=(), held_as=jnp.bfloat16):
    values = deviation * jax.random.normal(stream_key, extent, jnp.float32)
    if cuts:
        values = values * steps_of(stream_key, extent, cuts, -0.22, 0.18)
    return jnp.clip(values, -limit, limit).astype(held_as)


def setup_inputs(seed: int = 0, part: int = 0) -> dict:
    arg_keys = jax.random.split(jax.random.key(seed), 12)
    own_keys = jax.random.split(jax.random.fold_in(arg_keys[11], part), 12)
    pair_map = draw_pair_map(jax.random.fold_in(jax.random.fold_in(arg_keys[11], part), 71), part)
    chain_ids = jnp.searchsorted(jnp.cumsum(uneven_parts(own_keys[1], CHAINS, N, N // 4, 2)), jnp.arange(N), side="right").astype(jnp.int32)
    token_mask = touch_ends((jax.random.randint(own_keys[2], (N,), 0, 8) < 7).astype(jnp.int32), jax.random.fold_in(own_keys[2], 1), 0, 1)
    band_start = jax.random.randint(own_keys[3], (1,), 0, N - BAND + 1).astype(jnp.int32)
    chain_embed = bell_draw(arg_keys[4], (C,), 2.0, 8.0, (), jnp.float32)
    gain_in = jnp.clip(1.0 + 0.18 * jax.random.normal(arg_keys[5], (C,), jnp.float32), 0.1, 1.9)
    gain_out = jnp.clip(1.0 + 0.18 * jax.random.normal(arg_keys[6], (C,), jnp.float32), 0.1, 1.9)
    w_left = bell_draw(arg_keys[7], (C, 2 * C), C ** -0.5, 0.5, ((1, 2),))
    w_right = bell_draw(arg_keys[8], (C, 2 * C), C ** -0.5, 0.5, ((1, 2),))
    w_gate = bell_draw(arg_keys[9], (C, C), C ** -0.5, 0.5, ((1, 2),))
    w_out = bell_draw(arg_keys[10], (C, C), C ** -0.5, 0.5, ((1, 2),))
    return {"pair_map": pair_map, "chain_ids": chain_ids, "token_mask": token_mask, "band_start": band_start, "chain_embed": chain_embed, "gain_in": gain_in, "gain_out": gain_out, "w_left": w_left, "w_right": w_right, "w_gate": w_gate, "w_out": w_out}


norm_eps = 1e-05

def layer_norm(values, gain_vec):
    average = lax.optimization_barrier(jnp.mean(values, -1, keepdims=True))
    centered = values - average
    variance = lax.optimization_barrier(jnp.mean(centered * centered, -1, keepdims=True))
    return centered * lax.rsqrt(variance + norm_eps) * gain_vec

def normalize(block_rows, same_chain, chain_embed, gain_in):
    shifted = block_rows.astype(jnp.float32) + same_chain[..., None] * chain_embed
    return layer_norm(shifted, gain_in).astype(jnp.bfloat16)

def gated_proj(normed, weight, pair_weight):
    half_width = weight.shape[0]
    both_proj = jnp.dot(normed, weight, preferred_element_type=jnp.float32)
    gate_half = both_proj[..., :half_width]
    value_half = both_proj[..., half_width:]
    return (jax.nn.sigmoid(gate_half) * value_half * pair_weight[..., None]).astype(jnp.bfloat16)

def reference(pair_map, chain_ids, token_mask, band_start, chain_embed, gain_in, gain_out, w_left, w_right, w_gate, w_out):
    band_first = band_start[0].astype(jnp.int32)
    token_weight = token_mask.astype(jnp.float32)
    band_chain = lax.dynamic_slice_in_dim(chain_ids, band_first, BAND)
    band_mask = lax.dynamic_slice_in_dim(token_weight, band_first, BAND)
    block_total = N // ROWS_DEV

    def scan_step(running, block_index):
        row_first = (block_index * ROWS_DEV).astype(jnp.int32)
        row_block = lax.dynamic_slice_in_dim(pair_map, row_first, ROWS_DEV, 0)
        row_chain = lax.dynamic_slice_in_dim(chain_ids, row_first, ROWS_DEV)
        row_mask = lax.dynamic_slice_in_dim(token_weight, row_first, ROWS_DEV)
        same_chain = (row_chain[:, None] == chain_ids[None, :]).astype(jnp.float32)
        normed = normalize(row_block, same_chain, chain_embed, gain_in)
        left_proj = gated_proj(normed, w_left, row_mask[:, None] * token_weight[None, :])
        band_normed = lax.dynamic_slice_in_dim(normed, band_first, BAND, 1)
        right_proj = gated_proj(band_normed, w_right, row_mask[:, None] * band_mask[None, :])
        gate_values = jax.nn.sigmoid(jnp.dot(band_normed, w_gate, preferred_element_type=jnp.float32))
        running = running + jnp.einsum('kic,kjc->ijc', left_proj.astype(jnp.float32), right_proj.astype(jnp.float32))
        return (running, gate_values)
    start_total = jnp.zeros((N, BAND, C), jnp.float32)
    triangle, gate_blocks = lax.scan(scan_step, start_total, jnp.arange(block_total, dtype=jnp.int32))
    gate_values = gate_blocks.reshape(N, BAND, C)
    normed_out = layer_norm(triangle, gain_out).astype(jnp.bfloat16)
    projected = jnp.dot(normed_out, w_out, preferred_element_type=jnp.float32)
    return (gate_values * projected).astype(jnp.bfloat16)
```

```python
import functools

import jax
import jax.numpy as jnp
from jax import lax
from jax.experimental import pallas as pl
from jax.experimental.pallas import tpu as pltpu
from jax.sharding import PartitionSpec as P

BAND = 48
NORM_EPS = 1e-05
F32, BF16, I32 = jnp.float32, jnp.bfloat16, jnp.int32
LAST = (((1,), (1,)), ((), ()))


def layer_norm(values, gain):
    mean = jnp.mean(values, -1, keepdims=True)
    centered = values - mean
    var = jnp.mean(centered * centered, -1, keepdims=True)
    return centered * lax.rsqrt(var + NORM_EPS) * gain


def halves(own, other, first):
    return jnp.where(first, own, other), jnp.where(first, other, own)


def right_kernel(
    chain_s, mask_s, meta, own_band, other_band, chain_cols, embed, gain, w_own, w_other, row_mask, right_ref, gate_ref,
    normed_scr, right_scr,
):
    rows, band, width = own_band.shape
    both = 2 * rows
    start = meta[4]
    first = meta[1] == 0
    band_chain = chain_cols[pl.ds(start, band), :]
    emb, gn = embed[...], gain[...]
    for source, base, ref in ((0, meta[2], own_band), (1, meta[3], other_band)):
        for k in range(rows):
            same = band_chain == chain_s[base + k]
            shifted = ref[k].astype(F32) + jnp.where(same, emb, 0.0)
            keep = mask_s[base + k].astype(F32)
            row = (source * rows + k) * band
            normed_scr[row : row + band, :] = layer_norm(shifted, gn) * keep
    w_gate_half, w_value_half = halves(w_own[width : 2 * width, :], w_other[width : 2 * width, :], first)
    w_right = jnp.concatenate([w_gate_half, w_value_half], 0)
    half = width // 2
    low, high = halves(w_own[2 * width : 2 * width + half, :], w_other[2 * width : 2 * width + half, :], first)
    w_gate = jnp.concatenate([low, high], 0)
    mask_i = row_mask[...]
    for j in range(band):
        normed = normed_scr[pl.ds(j, both, stride=band), :].astype(BF16)
        proj = lax.dot_general(w_right, normed, LAST, preferred_element_type=F32)
        edge = jax.nn.sigmoid(proj[:width]) * proj[width:] * mask_s[start + j].astype(F32)
        right_scr[pl.ds(j, width, stride=band), 0:both] = edge
        gate = lax.dot_general(normed[0:rows], w_gate, LAST, preferred_element_type=F32)
        gate_ref[j] = jax.nn.sigmoid(gate) * mask_i
    right_ref[...] = right_scr[:, 0:both].reshape(width, band, both).astype(BF16)


def triangle_kernel(group, tile, out_type, chain_s, mask_s, meta, *refs):
    own = refs[:group]
    other = refs[group : 2 * group]
    chain_cols = refs[2 * group : 3 * group]
    embed, gain, w_own, w_other, right_ref = refs[3 * group : 3 * group + 5]
    outs = refs[3 * group + 5 : 4 * group + 5]
    left_scr, tri_scr = refs[4 * group + 5 :]
    width, band, both = right_ref.shape
    rows = both // 2
    size = own[0].shape[2]
    lanes = group * size
    step = pl.program_id(0)
    first = meta[1] == 0
    w_gate_half, w_value_half = halves(w_own[0:width, :], w_other[0:width, :], first)
    w_left = jnp.concatenate([w_gate_half, w_value_half], 0)
    chains = jnp.concatenate([ref[...] for ref in chain_cols], 0)
    emb, gn = embed[...], gain[...]

    def normed(source, k):
        base = meta[3] if source else meta[2]
        values = jnp.concatenate([ref[k, 0] for ref in (other if source else own)], 0)
        same = chains == chain_s[base + step * tile + k]
        return layer_norm(values.astype(F32) + jnp.where(same, emb, 0.0), gn).astype(BF16)

    for k in range(tile):
        pair = jnp.concatenate([normed(0, k), normed(1, k)], 0)
        proj = lax.dot_general(w_left, pair, LAST, preferred_element_type=F32)
        edge = jax.nn.sigmoid(proj[:width]) * proj[width:]
        at = step * tile + k
        left_scr[pl.ds(at, width, stride=both), :] = edge[:, :lanes]
        left_scr[pl.ds(at + rows, width, stride=both), :] = edge[:, lanes:]

    @pl.when(step == pl.num_programs(0) - 1)
    def _():
        unroll = 8

        def channels(block, carry):
            for u in range(unroll):
                c = block * unroll + u
                left = left_scr[pl.ds(pl.multiple_of(c * both, both), both), :].astype(BF16)
                tri = jnp.dot(right_ref[c], left, preferred_element_type=F32)
                tri_scr[pl.ds(pl.multiple_of(c * band, 8), band), :] = tri
            return carry

        lax.fori_loop(0, width // unroll, channels, 0)
        for j in range(band):
            turned = tri_scr[pl.ds(j, width, stride=band), :].T
            for b in range(group):
                outs[b][j] = turned[b * size : (b + 1) * size].astype(out_type)


def final_kernel(count, keep_ref, *refs):
    arrived = refs[:count]
    gate_ref, gain, w_own, w_other, nr_s, out_ref, scr = refs[count:]
    band, rows, width = keep_ref.shape
    half = width // 2
    low, high = halves(w_own[2 * width + half :, :], w_other[2 * width + half :, :], nr_s[1] == 0)
    w_out = jnp.concatenate([low, high], 0)
    total = keep_ref[...]
    for ref in arrived:
        total = total + ref[...].astype(F32)
    normed = layer_norm(total.reshape(band * rows, width), gain[...]).astype(BF16)
    projected = lax.dot_general(normed, w_out, LAST, preferred_element_type=F32)
    for j in range(band):
        scr[pl.ds(j, rows, stride=band), :] = projected[j * rows : (j + 1) * rows] * gate_ref[j]
    out_ref[...] = scr[...].reshape(rows, band, width).astype(BF16)


def body(pair_map, chain_ids, token_mask, band_start, chain_embed, gain_in, gain_out, w_left, w_right, w_gate, w_out):
    rows, tokens, width = pair_map.shape
    n_ax = lax.axis_size("ax")
    ax, nr = lax.axis_index("ax"), lax.axis_index("nr")
    band = BAND
    both = 2 * rows

    def swap_core(x):
        return lax.ppermute(x, "nr", [(0, 1), (1, 0)])

    def swap(x, bit):
        return lax.ppermute(x, "ax", [(s, s ^ bit) for s in range(n_ax)])

    start = band_start[0]
    own_row, other_row = (ax * 2 + nr) * rows, (ax * 2 + 1 - nr) * rows
    meta = jnp.stack([ax, nr, own_row, other_row, start]).astype(I32)

    w_own = jnp.concatenate([w_left.T, w_right.T, w_gate.T, w_out.T], 0)
    w_other = swap_core(w_own)
    own_band = lax.dynamic_slice_in_dim(pair_map, start, band, 1)
    other_band = swap_core(own_band)
    blocks = pair_map.reshape(rows, n_ax // 2, 2, 2, rows, width)

    def for_other_core(parity):
        part = lax.dynamic_slice(
            blocks, (0, 0, parity, 1 - nr, 0, 0), (rows, n_ax // 2, 1, 1, rows, width)
        ).reshape(rows, n_ax // 2, rows, width)
        return swap_core(part)

    other_far, other_near = for_other_core(1 - (ax & 1)), for_other_core(ax & 1)
    own_blocks = pair_map.reshape(rows, tokens // rows, rows, width)
    chain_cols = jnp.broadcast_to(chain_ids[:, None], (tokens, 128))
    row_mask = jnp.broadcast_to(
        lax.dynamic_slice_in_dim(token_mask, own_row, rows).astype(F32)[:, None], (rows, width)
    )
    embed, gain, gain_o = chain_embed[None], gain_in[None], gain_out[None]

    vmem = pl.BlockSpec(memory_space=pltpu.VMEM)
    right, gate = pl.pallas_call(
        right_kernel,
        grid_spec=pltpu.PrefetchScalarGridSpec(
            num_scalar_prefetch=3,
            grid=(),
            in_specs=[vmem] * 8,
            out_specs=[vmem] * 2,
            scratch_shapes=[pltpu.VMEM((both * band, width), F32), pltpu.VMEM((width * band, 128), F32)],
        ),
        out_shape=[
            jax.ShapeDtypeStruct((width, band, both), BF16),
            jax.ShapeDtypeStruct((band, rows, width), F32),
        ],
        compiler_params=pltpu.CompilerParams(vmem_limit_bytes=40 << 20),
        cost_estimate=pl.CostEstimate(flops=4 * 10**9, bytes_accessed=2 * 10**6, transcendentals=0),
        name="right",
    )(chain_ids, token_mask, meta, own_band, other_band, chain_cols, embed, gain, w_own, w_other, row_mask)

    def triangle(relative, other_part, out_type):
        group = len(relative)
        tile = 8
        row_specs, part_specs, chain_specs = [], [], []
        for r in relative:
            row_specs.append(
                pl.BlockSpec((tile, 1, rows, width), lambda t, c, m, meta, r=r: (t, (meta[0] ^ r) * 2 + meta[1], 0, 0))
            )
            part_specs.append(
                pl.BlockSpec((tile, 1, rows, width), lambda t, c, m, meta, r=r: (t, (meta[0] ^ r) >> 1, 0, 0))
            )
            chain_specs.append(pl.BlockSpec((rows, 128), lambda t, c, m, meta, r=r: ((meta[0] ^ r) * 2 + meta[1], 0)))
        whole = lambda shape: pl.BlockSpec(shape, lambda t, c, m, meta: (0,) * len(shape))
        out_shape = (band, rows, width)
        return pl.pallas_call(
            functools.partial(triangle_kernel, group, tile, out_type),
            grid_spec=pltpu.PrefetchScalarGridSpec(
                num_scalar_prefetch=3,
                grid=(rows // tile,),
                in_specs=row_specs
                + part_specs
                + chain_specs
                + [whole((1, width)), whole((1, width)), whole(w_own.shape), whole(w_own.shape), whole((width, band, both))],
                out_specs=[whole(out_shape)] * group,
                scratch_shapes=[
                    pltpu.VMEM((width * both, group * rows), F32),
                    pltpu.VMEM((width * band, group * rows), F32),
                ],
            ),
            out_shape=[jax.ShapeDtypeStruct(out_shape, out_type)] * group,
            compiler_params=pltpu.CompilerParams(vmem_limit_bytes=48 << 20),
            cost_estimate=pl.CostEstimate(flops=8 * 10**9, bytes_accessed=4 * 10**6, transcendentals=0),
            name="triangle",
        )(
            chain_ids, token_mask, meta, *([own_blocks] * group), *([other_part] * group), *([chain_cols] * group),
            embed, gain, w_own, w_other, right,
        )

    size = min(128 // rows, n_ax // 2)
    odd, even = list(range(n_ax - 1, 0, -2)), list(range(n_ax - 2, -1, -2))
    parts = {}
    arrived = {r: [] for r in even}
    for at in range(0, len(odd), size):
        group = odd[at : at + size]
        for r, part in zip(group, triangle(group, other_far, BF16)):
            arrived[r - 1].append(swap(part, 1))
    for at in range(0, len(even), size):
        group = even[at : at + size]
        for r, part in zip(group, triangle(group, other_near, F32)):
            parts[r] = part
    for r in even[:-1]:
        total = parts[r]
        for piece in arrived[r]:
            total = total + piece.astype(F32)
        bit = r & -r
        arrived[r - bit].append(swap(total.astype(BF16), bit))

    pieces = arrived[0]
    return pl.pallas_call(
        functools.partial(final_kernel, len(pieces)),
        in_specs=[vmem] * (len(pieces) + 5) + [pl.BlockSpec(memory_space=pltpu.SMEM)],
        out_specs=vmem,
        out_shape=jax.ShapeDtypeStruct((rows, band, width), BF16),
        scratch_shapes=[pltpu.VMEM((rows * band, width), F32)],
        compiler_params=pltpu.CompilerParams(vmem_limit_bytes=32 << 20),
        cost_estimate=pl.CostEstimate(flops=10**9, bytes_accessed=3 * 10**6, transcendentals=0),
        name="final",
    )(parts[0], *pieces, gate, gain_o, w_own, w_other, meta)


def solution(mesh):
    in_specs = (
        P(("grp", "ax", "nr"), None, None),
        P("grp"),
        P("grp"),
        P("grp"),
        P(),
        P(),
        P(),
        P(None, "nr"),
        P(None, "nr"),
        P(None, "nr"),
        P(None, "nr"),
    )
    out_specs = P(("grp", "ax", "nr"), None, None)
    return jax.shard_map(body, mesh=mesh, in_specs=in_specs, out_specs=out_specs, check_vma=False)
```

```python
import functools

import jax
import jax.numpy as jnp
from jax import lax
from jax.experimental import pallas as pl
from jax.experimental.pallas import tpu as pltpu
from jax.sharding import PartitionSpec as P

BAND = 48
NORM_EPS = 1e-05
GROUP = 4
F32, BF16, I32 = jnp.float32, jnp.bfloat16, jnp.int32
LAST = (((1,), (1,)), ((), ()))


def layer_norm(values, gain):
    mean = jnp.mean(values, -1, keepdims=True)
    centered = values - mean
    var = jnp.mean(centered * centered, -1, keepdims=True)
    return centered * lax.rsqrt(var + NORM_EPS) * gain


def place_of(label, ax, nr):
    swapped = (label & ~3) | ((label & 1) << 1) | ((label >> 1) & 1)
    return ax ^ (label + (swapped - label) * nr)


def pack_kernel(far_labels, near_labels, meta, pairs, weights, first, far, near, sems):
    window = first.shape[1] - 16
    ax, other = meta[0], 1 - meta[1]
    base = pl.multiple_of(meta[5], 16)
    copies = [pltpu.make_async_copy(pairs.at[:, pl.ds(base, window), :], first.at[:, 0:window, :], sems.at[0])]
    size = far.shape[2]
    for part, labels in ((far, far_labels), (near, near_labels)):
        for m, label in enumerate(labels):
            block = place_of(label, ax, other) * 2 + other
            rows = pl.ds(pl.multiple_of(block * size, size), size)
            copies.append(pltpu.make_async_copy(pairs.at[:, rows, :], part.at[:, m], sems.at[len(copies)]))
    for copy in copies:
        copy.start()
    half = weights.shape[0] // 3
    turned = [weights[n * half : (n + 1) * half].astype(F32).T.astype(BF16) for n in range(2)] + [weights[2 * half :]]
    turned = jnp.concatenate(turned + turned[:1], 0)
    for row in range(first.shape[0]):
        first[row, window:, :] = turned[row * 16 : row * 16 + 16]
    for copy in copies:
        copy.wait()


def right_kernel(
    chain_s, mask_s, meta, own, other, chain_cols, embed, gain, right_ref, w_left_ref, w_gate_ref, w_out_ref, band_ref,
    normed_scr, right_scr,
):
    rows, window, width = own.shape
    window -= 16
    band = BAND
    both = 2 * rows
    pitch, turn = window + 8, band + 8
    base = pl.multiple_of(meta[5], 16)
    offset = meta[4] - meta[5]
    first = meta[1] == 0
    chains = chain_cols[pl.ds(base, window), :]
    emb, gn = embed[...], gain[...]
    w_own = own[:, window:, :].reshape(rows * 16, width)
    w_other = other[:, window:, :].reshape(rows * 16, width)
    low, high = jnp.where(first, w_own, w_other), jnp.where(first, w_other, w_own)

    def weight(start, size):
        return jnp.concatenate([low[start : start + size], high[start : start + size]], 0)

    w_left_ref[...] = weight(0, width)
    w_right = weight(width, width)
    w_gate_ref[...] = weight(2 * width, width // 2)
    w_out_ref[...] = weight(2 * width + width // 2, width // 2)
    for source, start, ref in ((0, meta[2], own), (1, meta[3], other)):
        for k in range(rows):
            same = chains == chain_s[start + k]
            shifted = ref[k, 0:window].astype(F32) + jnp.where(same, emb, 0.0)
            keep = mask_s[start + k].astype(F32)
            row = (source * rows + k) * pitch
            normed_scr[row : row + window, :] = layer_norm(shifted, gn * keep)
    channel = lax.broadcasted_iota(I32, (width, 2 * both), 0)
    lane = lax.broadcasted_iota(I32, (width, 2 * both), 1)
    spread = ((channel & 1) == lane // both).astype(F32)
    for j in range(0, band, 2):
        normed = [normed_scr[pl.ds(offset + j + u, both, stride=pitch), :].astype(BF16) for u in range(2)]
        doubled = jnp.concatenate([normed[0], normed[0], normed[1], normed[1]], 0)
        proj = lax.dot_general(w_right, doubled, LAST, preferred_element_type=F32)
        edge = jax.nn.sigmoid(proj[:width]) * proj[width:]
        for u in range(2):
            keep = spread * mask_s[meta[4] + j + u].astype(F32)
            right_scr[pl.ds(j + u, width, stride=turn), :] = edge[:, u * 2 * both : (u + 1) * 2 * both] * keep
            band_ref[j + u] = normed[u][0:rows]
    for g in range(width // 2):
        pair = [right_scr[(2 * g + u) * turn : (2 * g + u) * turn + band, :] for u in range(2)]
        right_ref[g] = jnp.concatenate(pair, 0).astype(BF16)


def gate_kernel(band_ref, w_gate, mask_i, gate_ref):
    band, rows, width = band_ref.shape
    gate = lax.dot_general(band_ref[...].reshape(band * rows, width), w_gate[...], LAST, preferred_element_type=F32)
    gate_ref[...] = jax.nn.sigmoid(gate).reshape(band, rows, width) * mask_i[...][None]


def triangle_kernel(group, tile, stack, out_type, chain_s, mask_s, meta, *refs):
    own = refs[:group]
    other = refs[group : 2 * group]
    chain_cols = refs[2 * group : 3 * group]
    embed, gain, w_left_ref, right_ref = refs[3 * group : 3 * group + 4]
    outs = refs[3 * group + 4 : -2]
    left_scr, tri_scr = refs[-2:]
    pairs, wide, both2 = right_ref.shape
    width, band, both = pairs * 2, wide // 2, both2 // 2
    rows = both // 2
    pitch, turn = both + 8, band + 8
    size = own[0].shape[2]
    lanes = group * size
    step = pl.program_id(0)
    w_left = w_left_ref[...]
    chains = jnp.concatenate([ref[...] for ref in chain_cols], 0)
    emb, gn = embed[...], gain[...]

    def normed(source, k):
        base = meta[3] if source else meta[2]
        values = jnp.concatenate([ref[k, 0] for ref in (other if source else own)], 0)
        same = chains == chain_s[base + step * tile + k]
        return layer_norm(values.astype(F32) + jnp.where(same, emb, 0.0), gn).astype(BF16)

    for k in range(tile):
        pair = jnp.concatenate([normed(0, k), normed(1, k)], 0)
        proj = lax.dot_general(w_left, pair, LAST, preferred_element_type=F32)
        edge = jax.nn.sigmoid(proj[:width]) * proj[width:]
        at = step * tile + k
        left_scr[pl.ds(at, width, stride=pitch), :] = edge[:, :lanes]
        left_scr[pl.ds(at + rows, width, stride=pitch), :] = edge[:, lanes:]

    @pl.when(step == pl.num_programs(0) - 1)
    def _():
        for g in range(pairs):
            left = jnp.concatenate([left_scr[c * pitch : c * pitch + both, :] for c in (2 * g, 2 * g + 1)], 0)
            tri = jnp.dot(right_ref[g], left.astype(BF16), preferred_element_type=F32)
            tri_scr[2 * g * turn : 2 * g * turn + band, :] = tri[:band]
            tri_scr[(2 * g + 1) * turn : (2 * g + 1) * turn + band, :] = tri[band:]
        for j in range(band):
            turned = tri_scr[pl.ds(j, width, stride=turn), :].T
            for b in range(group):
                outs[b // stack][b % stack * band + j] = turned[b * size : (b + 1) * size].astype(out_type)


def final_kernel(starts, *refs):
    pieces = refs[: len(starts)]
    gate_ref, gain, w_out, out_ref, scr = refs[len(starts) :]
    band, rows, width = gate_ref.shape
    turn = band + 8
    total = pieces[0][...]
    for ref, start in zip(pieces[1:], starts[1:]):
        total = total + ref[start : start + band].astype(F32)
    normed = layer_norm(total.reshape(band * rows, width), gain[...]).astype(BF16)
    projected = lax.dot_general(normed, w_out[...], LAST, preferred_element_type=F32)
    for j in range(band):
        scr[pl.ds(j, rows, stride=turn), :] = projected[j * rows : (j + 1) * rows] * gate_ref[j]
    for i in range(rows):
        out_ref[i] = scr[i * turn : i * turn + band, :].astype(BF16)


def body(pair_map, chain_ids, token_mask, band_start, chain_embed, gain_in, gain_out, w_left, w_right, w_gate, w_out):
    rows, tokens, width = pair_map.shape
    n_ax = lax.axis_size("ax")
    ax, nr = lax.axis_index("ax"), lax.axis_index("nr")
    band, tile = BAND, 8
    odd, even = list(range(n_ax - 1, 0, -2)), list(range(n_ax - 2, -1, -2))
    both = 2 * rows
    window = band + 16
    vmem = pl.BlockSpec(memory_space=pltpu.VMEM)
    smem = pl.BlockSpec(memory_space=pltpu.SMEM)
    hbm = pl.BlockSpec(memory_space=pltpu.HBM)

    def swap_core(x):
        return lax.ppermute(x, "nr", [(0, 1), (1, 0)])

    def swap(x, bit):
        pairs = []
        for s in range(n_ax):
            for core in range(2):
                pairs.append((s * 2 + core, place_of(bit, s, core) * 2 + core))
        return lax.ppermute(x, ("ax", "nr"), pairs)

    def after(x, done):
        return lax.optimization_barrier((x, done))[0]

    start = band_start[0]
    own_row, other_row = (ax * 2 + nr) * rows, (ax * 2 + 1 - nr) * rows
    meta = jnp.stack([ax, nr, own_row, other_row, start, jnp.minimum(start // 16 * 16, tokens - window)]).astype(I32)

    part_shape = jax.ShapeDtypeStruct((rows, n_ax // 2, rows, width), BF16)
    weights = jnp.concatenate([w_left, w_right, w_gate.T, w_out.T], 0)
    own_first, far, near = pl.pallas_call(
        functools.partial(pack_kernel, odd, even),
        in_specs=[smem, hbm, vmem],
        out_specs=[vmem] * 3,
        out_shape=[jax.ShapeDtypeStruct((rows, window + 16, width), BF16), part_shape, part_shape],
        scratch_shapes=[pltpu.SemaphoreType.DMA((1 + n_ax,))],
        compiler_params=pltpu.CompilerParams(vmem_limit_bytes=10 << 20),
        name="pack",
    )(meta, pair_map, weights)
    other_first, other_far, other_near = swap_core(own_first), swap_core(far), swap_core(near)
    own_blocks = pair_map.reshape(rows, tokens // rows, rows, width)
    chain_cols = jnp.broadcast_to(chain_ids[:, None], (tokens, 128))
    row_mask = jnp.broadcast_to(
        lax.dynamic_slice_in_dim(token_mask, own_row, rows).astype(F32)[:, None], (rows, width)
    )
    embed, gain, gain_o = chain_embed[None], gain_in[None], gain_out[None]

    right, w_left, w_gate, w_out, own_band = pl.pallas_call(
        right_kernel,
        grid_spec=pltpu.PrefetchScalarGridSpec(
            num_scalar_prefetch=3,
            grid=(),
            in_specs=[vmem] * 5,
            out_specs=[vmem] * 5,
            scratch_shapes=[
                pltpu.VMEM((both * (window + 8), width), F32),
                pltpu.VMEM((width * (band + 8), 2 * both), F32),
            ],
        ),
        out_shape=[
            jax.ShapeDtypeStruct((width // 2, 2 * band, 2 * both), BF16),
            jax.ShapeDtypeStruct((2 * width, width), BF16),
            jax.ShapeDtypeStruct((width, width), BF16),
            jax.ShapeDtypeStruct((width, width), BF16),
            jax.ShapeDtypeStruct((band, rows, width), BF16),
        ],
        compiler_params=pltpu.CompilerParams(vmem_limit_bytes=18 << 20),
        cost_estimate=pl.CostEstimate(flops=4 * 10**9, bytes_accessed=2 * 10**6, transcendentals=0),
        name="right",
    )(chain_ids, token_mask, meta, own_first, other_first, chain_cols, embed, gain)

    def triangle(labels, other_part, out_type, stack, scalars):
        group = len(labels)
        row_specs, part_specs, chain_specs = [], [], []
        for v in labels:
            row_specs.append(
                pl.BlockSpec(
                    (tile, 1, rows, width),
                    lambda t, c, m, meta, v=v: (t, place_of(v, meta[0], meta[1]) * 2 + meta[1], 0, 0),
                )
            )
            at = (odd if v & 1 else even).index(v)
            part_specs.append(pl.BlockSpec((tile, 1, rows, width), lambda t, c, m, meta, at=at: (t, at, 0, 0)))
            chain_specs.append(
                pl.BlockSpec((rows, 128), lambda t, c, m, meta, v=v: (place_of(v, meta[0], meta[1]) * 2 + meta[1], 0))
            )
        whole = lambda shape: pl.BlockSpec(shape, lambda t, c, m, meta: (0,) * len(shape))
        out_shape = (stack * band, rows, width)
        return pl.pallas_call(
            functools.partial(triangle_kernel, group, tile, stack, out_type),
            grid_spec=pltpu.PrefetchScalarGridSpec(
                num_scalar_prefetch=3,
                grid=(rows // tile,),
                in_specs=row_specs
                + part_specs
                + chain_specs
                + [whole((1, width)), whole((1, width)), whole(w_left.shape), whole(right.shape)],
                out_specs=[whole(out_shape)] * (group // stack),
                scratch_shapes=[
                    pltpu.VMEM((width * (both + 8), group * rows), F32),
                    pltpu.VMEM((width * (band + 8), group * rows), F32),
                ],
            ),
            out_shape=[jax.ShapeDtypeStruct(out_shape, out_type)] * (group // stack),
            compiler_params=pltpu.CompilerParams(vmem_limit_bytes=28 << 20),
            cost_estimate=pl.CostEstimate(flops=8 * 10**9, bytes_accessed=4 * 10**6, transcendentals=0),
            name="triangle",
        )(
            chain_ids, token_mask, scalars, *([own_blocks] * group), *([other_part] * group), *([chain_cols] * group),
            embed, gain, w_left, right,
        )

    size = GROUP
    pairs, kept = [], {}
    for at in range(0, len(odd), size):
        pairs += triangle(odd[at : at + size], other_far, BF16, 2, meta)
    for at in range(0, len(even), size):
        labels = even[at : at + size]
        kept.update(zip(labels, triangle(labels, other_near, F32, 1, after(meta, pairs[-1]))))
    gate = pl.pallas_call(
        gate_kernel,
        in_specs=[vmem] * 3,
        out_specs=vmem,
        out_shape=jax.ShapeDtypeStruct((band, rows, width), F32),
        compiler_params=pltpu.CompilerParams(vmem_limit_bytes=10 << 20),
        cost_estimate=pl.CostEstimate(flops=10**9, bytes_accessed=2 * 10**6, transcendentals=0),
        name="gate",
    )(own_band, w_gate, after(row_mask, kept[0]))

    arrived = {v: [(kept[v], 0)] for v in even}

    def send_pair(n, x):
        moved = swap(x, 1)
        for m in range(2):
            arrived[odd[2 * n + m] - 1].append((moved, m * band))

    def send(v):
        total = sum(piece[start : start + band].astype(F32) for piece, start in arrived[v])
        bit = v & -v
        arrived[v - bit].append((swap(total.astype(BF16), bit), 0))
        return arrived[v - bit][-1][0]

    send_pair(0, pairs[0])
    first_sent = send(even[0])
    for n in range(1, len(pairs)):
        send_pair(n, after(pairs[n], first_sent))
    for v in even[1:-1]:
        send(v)

    pieces, starts = zip(*arrived[0])
    return pl.pallas_call(
        functools.partial(final_kernel, starts),
        in_specs=[vmem] * (len(pieces) + 3),
        out_specs=vmem,
        out_shape=jax.ShapeDtypeStruct((rows, band, width), BF16),
        scratch_shapes=[pltpu.VMEM((rows * (band + 8), width), F32)],
        compiler_params=pltpu.CompilerParams(vmem_limit_bytes=14 << 20),
        cost_estimate=pl.CostEstimate(flops=10**9, bytes_accessed=3 * 10**6, transcendentals=0),
        name="final",
    )(*pieces, gate, gain_o, w_out)


def solution(mesh):
    in_specs = (
        P(("grp", "ax", "nr"), None, None),
        P("grp"),
        P("grp"),
        P("grp"),
        P(),
        P(),
        P(),
        P(None, "nr"),
        P(None, "nr"),
        P(None, "nr"),
        P(None, "nr"),
    )
    out_specs = P(("grp", "ax", "nr"), None, None)
    return jax.shard_map(body, mesh=mesh, in_specs=in_specs, out_specs=out_specs, check_vma=False)
```

```python
import functools

import jax
import jax.numpy as jnp
from jax import lax
from jax.experimental import pallas as pl
from jax.experimental.pallas import tpu as pltpu
from jax.sharding import PartitionSpec as P

BAND = 48
NORM_EPS = 1e-05
STACKS = (2, 1, 1)
GROUP = 4
F32, BF16, I32 = jnp.float32, jnp.bfloat16, jnp.int32
LAST = (((1,), (1,)), ((), ()))


def layer_norm(values, gain):
    mean = jnp.mean(values, -1, keepdims=True)
    centered = values - mean
    var = jnp.mean(centered * centered, -1, keepdims=True)
    return centered * lax.rsqrt(var + NORM_EPS) * gain


def place_of(label, ax, nr):
    swapped = (label & ~3) | ((label & 1) << 1) | ((label >> 1) & 1)
    return ax ^ (label + (swapped - label) * nr)


def pack_kernel(far_labels, near_labels, meta, pairs, weights, first, far, near, sems):
    window = first.shape[1] - 16
    ax, other = meta[0], 1 - meta[1]
    base = pl.multiple_of(meta[5], 16)
    copies = [pltpu.make_async_copy(pairs.at[:, pl.ds(base, window), :], first.at[:, 0:window, :], sems.at[0])]
    size = far.shape[2]
    for part, labels in ((far, far_labels), (near, near_labels)):
        for m, label in enumerate(labels):
            block = place_of(label, ax, other) * 2 + other
            rows = pl.ds(pl.multiple_of(block * size, size), size)
            copies.append(pltpu.make_async_copy(pairs.at[:, rows, :], part.at[:, m], sems.at[len(copies)]))
    for copy in copies:
        copy.start()
    half = weights.shape[0] // 3
    turned = [weights[n * half : (n + 1) * half].astype(F32).T.astype(BF16) for n in range(2)] + [weights[2 * half :]]
    turned = jnp.concatenate(turned + turned[:1], 0)
    for row in range(first.shape[0]):
        first[row, window:, :] = turned[row * 16 : row * 16 + 16]
    for copy in copies:
        copy.wait()


def right_kernel(
    chain_s, mask_s, meta, own, other, chain_cols, embed, gain, right_ref, w_left_ref, w_gate_ref, w_out_ref, band_ref,
    normed_scr, right_scr,
):
    rows, window, width = own.shape
    window -= 16
    band = BAND
    both = 2 * rows
    pitch, turn = window + 8, band + 8
    base = pl.multiple_of(meta[5], 16)
    offset = meta[4] - meta[5]
    first = meta[1] == 0
    chains = chain_cols[pl.ds(base, window), :]
    emb, gn = embed[...], gain[...]
    w_own = own[:, window:, :].reshape(rows * 16, width)
    w_other = other[:, window:, :].reshape(rows * 16, width)
    low, high = jnp.where(first, w_own, w_other), jnp.where(first, w_other, w_own)

    def weight(start, size):
        return jnp.concatenate([low[start : start + size], high[start : start + size]], 0)

    w_left_ref[...] = weight(0, width)
    w_right = weight(width, width)
    w_gate_ref[...] = weight(2 * width, width // 2)
    w_out_ref[...] = weight(2 * width + width // 2, width // 2)
    for source, start, ref in ((0, meta[2], own), (1, meta[3], other)):
        for k in range(rows):
            same = chains == chain_s[start + k]
            shifted = ref[k, 0:window].astype(F32) + jnp.where(same, emb, 0.0)
            keep = mask_s[start + k].astype(F32)
            row = (source * rows + k) * pitch
            normed_scr[row : row + window, :] = layer_norm(shifted, gn * keep)
    channel = lax.broadcasted_iota(I32, (width, 2 * both), 0)
    lane = lax.broadcasted_iota(I32, (width, 2 * both), 1)
    spread = ((channel & 1) == lane // both).astype(F32)
    for j in range(0, band, 2):
        normed = [normed_scr[pl.ds(offset + j + u, both, stride=pitch), :].astype(BF16) for u in range(2)]
        doubled = jnp.concatenate([normed[0], normed[0], normed[1], normed[1]], 0)
        proj = lax.dot_general(w_right, doubled, LAST, preferred_element_type=F32)
        edge = jax.nn.sigmoid(proj[:width]) * proj[width:]
        for u in range(2):
            keep = spread * mask_s[meta[4] + j + u].astype(F32)
            right_scr[pl.ds(j + u, width, stride=turn), :] = edge[:, u * 2 * both : (u + 1) * 2 * both] * keep
            band_ref[j + u] = normed[u][0:rows]
    for g in range(width // 2):
        pair = [right_scr[(2 * g + u) * turn : (2 * g + u) * turn + band, :] for u in range(2)]
        right_ref[g] = jnp.concatenate(pair, 0).astype(BF16)


def gate_kernel(band_ref, w_gate, mask_i, gate_ref):
    band, rows, width = band_ref.shape
    gate = lax.dot_general(band_ref[...].reshape(band * rows, width), w_gate[...], LAST, preferred_element_type=F32)
    gate_ref[...] = jax.nn.sigmoid(gate).reshape(band, rows, width) * mask_i[...][None]


def triangle_kernel(group, tile, stacks, out_type, chain_s, mask_s, meta, *refs):
    own = refs[:group]
    other = refs[group : 2 * group]
    chain_cols = refs[2 * group : 3 * group]
    embed, gain, w_left_ref, right_ref = refs[3 * group : 3 * group + 4]
    outs = refs[3 * group + 4 : -2]
    slots = [(n, m) for n, stack in enumerate(stacks) for m in range(stack)]
    left_scr, tri_scr = refs[-2:]
    pairs, wide, both2 = right_ref.shape
    width, band, both = pairs * 2, wide // 2, both2 // 2
    rows = both // 2
    pitch, turn = both + 8, band + 8
    size = own[0].shape[2]
    lanes = group * size
    step = pl.program_id(0)
    w_left = w_left_ref[...]
    chains = jnp.concatenate([ref[...] for ref in chain_cols], 0)
    emb, gn = embed[...], gain[...]

    def normed(source, k):
        base = meta[3] if source else meta[2]
        values = jnp.concatenate([ref[k, 0] for ref in (other if source else own)], 0)
        same = chains == chain_s[base + step * tile + k]
        return layer_norm(values.astype(F32) + jnp.where(same, emb, 0.0), gn).astype(BF16)

    for k in range(tile):
        pair = jnp.concatenate([normed(0, k), normed(1, k)], 0)
        proj = lax.dot_general(w_left, pair, LAST, preferred_element_type=F32)
        edge = jax.nn.sigmoid(proj[:width]) * proj[width:]
        at = step * tile + k
        left_scr[pl.ds(at, width, stride=pitch), :] = edge[:, :lanes]
        left_scr[pl.ds(at + rows, width, stride=pitch), :] = edge[:, lanes:]

    @pl.when(step == pl.num_programs(0) - 1)
    def _():
        for g in range(pairs):
            left = jnp.concatenate([left_scr[c * pitch : c * pitch + both, :] for c in (2 * g, 2 * g + 1)], 0)
            tri = jnp.dot(right_ref[g], left.astype(BF16), preferred_element_type=F32)
            tri_scr[2 * g * turn : 2 * g * turn + band, :] = tri[:band]
            tri_scr[(2 * g + 1) * turn : (2 * g + 1) * turn + band, :] = tri[band:]
        for j in range(band):
            turned = tri_scr[pl.ds(j, width, stride=turn), :].T
            for b in range(group):
                outs[slots[b][0]][slots[b][1] * band + j] = turned[b * size : (b + 1) * size].astype(out_type)


def final_kernel(starts, *refs):
    pieces = refs[: len(starts)]
    gate_ref, gain, w_out, out_ref, scr = refs[len(starts) :]
    band, rows, width = gate_ref.shape
    turn = band + 8
    total = pieces[0][...]
    for ref, start in zip(pieces[1:], starts[1:]):
        total = total + ref[start : start + band].astype(F32)
    normed = layer_norm(total.reshape(band * rows, width), gain[...]).astype(BF16)
    projected = lax.dot_general(normed, w_out[...], LAST, preferred_element_type=F32)
    for j in range(band):
        scr[pl.ds(j, rows, stride=turn), :] = projected[j * rows : (j + 1) * rows] * gate_ref[j]
    for i in range(rows):
        out_ref[i] = scr[i * turn : i * turn + band, :].astype(BF16)


def body(pair_map, chain_ids, token_mask, band_start, chain_embed, gain_in, gain_out, w_left, w_right, w_gate, w_out):
    rows, tokens, width = pair_map.shape
    n_ax = lax.axis_size("ax")
    ax, nr = lax.axis_index("ax"), lax.axis_index("nr")
    band, tile = BAND, 8
    odd, even = list(range(n_ax - 1, 0, -2)), list(range(n_ax - 2, -1, -2))
    both = 2 * rows
    window = band + 16
    vmem = pl.BlockSpec(memory_space=pltpu.VMEM)
    smem = pl.BlockSpec(memory_space=pltpu.SMEM)
    hbm = pl.BlockSpec(memory_space=pltpu.HBM)

    def swap_core(x):
        return lax.ppermute(x, "nr", [(0, 1), (1, 0)])

    def swap(x, bit):
        pairs = []
        for s in range(n_ax):
            for core in range(2):
                pairs.append((s * 2 + core, place_of(bit, s, core) * 2 + core))
        return lax.ppermute(x, ("ax", "nr"), pairs)

    def after(x, done):
        return lax.optimization_barrier((x, done))[0]

    start = band_start[0]
    own_row, other_row = (ax * 2 + nr) * rows, (ax * 2 + 1 - nr) * rows
    meta = jnp.stack([ax, nr, own_row, other_row, start, jnp.minimum(start // 16 * 16, tokens - window)]).astype(I32)

    part_shape = jax.ShapeDtypeStruct((rows, n_ax // 2, rows, width), BF16)
    weights = jnp.concatenate([w_left, w_right, w_gate.T, w_out.T], 0)
    own_first, far, near = pl.pallas_call(
        functools.partial(pack_kernel, odd, even),
        in_specs=[smem, hbm, vmem],
        out_specs=[vmem] * 3,
        out_shape=[jax.ShapeDtypeStruct((rows, window + 16, width), BF16), part_shape, part_shape],
        scratch_shapes=[pltpu.SemaphoreType.DMA((1 + n_ax,))],
        compiler_params=pltpu.CompilerParams(vmem_limit_bytes=10 << 20),
        name="pack",
    )(meta, pair_map, weights)
    other_first = swap_core(own_first)
    other_far = swap_core(after(far, other_first))
    own_blocks = pair_map.reshape(rows, tokens // rows, rows, width)
    chain_cols = jnp.broadcast_to(chain_ids[:, None], (tokens, 128))
    row_mask = jnp.broadcast_to(
        lax.dynamic_slice_in_dim(token_mask, own_row, rows).astype(F32)[:, None], (rows, width)
    )
    embed, gain, gain_o = chain_embed[None], gain_in[None], gain_out[None]

    right, w_left, w_gate, w_out, own_band = pl.pallas_call(
        right_kernel,
        grid_spec=pltpu.PrefetchScalarGridSpec(
            num_scalar_prefetch=3,
            grid=(),
            in_specs=[vmem] * 5,
            out_specs=[vmem] * 5,
            scratch_shapes=[
                pltpu.VMEM((both * (window + 8), width), F32),
                pltpu.VMEM((width * (band + 8), 2 * both), F32),
            ],
        ),
        out_shape=[
            jax.ShapeDtypeStruct((width // 2, 2 * band, 2 * both), BF16),
            jax.ShapeDtypeStruct((2 * width, width), BF16),
            jax.ShapeDtypeStruct((width, width), BF16),
            jax.ShapeDtypeStruct((width, width), BF16),
            jax.ShapeDtypeStruct((band, rows, width), BF16),
        ],
        compiler_params=pltpu.CompilerParams(vmem_limit_bytes=18 << 20),
        cost_estimate=pl.CostEstimate(flops=4 * 10**9, bytes_accessed=2 * 10**6, transcendentals=0),
        name="right",
    )(chain_ids, token_mask, meta, own_first, other_first, chain_cols, embed, gain)

    other_near = swap_core(after(near, right))

    def triangle(labels, other_part, out_type, stacks, scalars):
        group = len(labels)
        row_specs, part_specs, chain_specs = [], [], []
        for v in labels:
            row_specs.append(
                pl.BlockSpec(
                    (tile, 1, rows, width),
                    lambda t, c, m, meta, v=v: (t, place_of(v, meta[0], meta[1]) * 2 + meta[1], 0, 0),
                )
            )
            at = (odd if v & 1 else even).index(v)
            part_specs.append(pl.BlockSpec((tile, 1, rows, width), lambda t, c, m, meta, at=at: (t, at, 0, 0)))
            chain_specs.append(
                pl.BlockSpec((rows, 128), lambda t, c, m, meta, v=v: (place_of(v, meta[0], meta[1]) * 2 + meta[1], 0))
            )
        whole = lambda shape: pl.BlockSpec(shape, lambda t, c, m, meta: (0,) * len(shape))
        out_shapes = [(stack * band, rows, width) for stack in stacks]
        return pl.pallas_call(
            functools.partial(triangle_kernel, group, tile, stacks, out_type),
            grid_spec=pltpu.PrefetchScalarGridSpec(
                num_scalar_prefetch=3,
                grid=(rows // tile,),
                in_specs=row_specs
                + part_specs
                + chain_specs
                + [whole((1, width)), whole((1, width)), whole(w_left.shape), whole(right.shape)],
                out_specs=[whole(shape) for shape in out_shapes],
                scratch_shapes=[
                    pltpu.VMEM((width * (both + 8), group * rows), F32),
                    pltpu.VMEM((width * (band + 8), group * rows), F32),
                ],
            ),
            out_shape=[jax.ShapeDtypeStruct(shape, out_type) for shape in out_shapes],
            compiler_params=pltpu.CompilerParams(vmem_limit_bytes=28 << 20),
            cost_estimate=pl.CostEstimate(flops=8 * 10**9, bytes_accessed=4 * 10**6, transcendentals=0),
            name="triangle",
        )(
            chain_ids, token_mask, scalars, *([own_blocks] * group), *([other_part] * group), *([chain_cols] * group),
            embed, gain, w_left, right,
        )

    size = GROUP
    far_stacks, kept = [], {}
    for at in range(0, len(odd), size):
        outs = triangle(odd[at : at + size], other_far, BF16, STACKS, meta)
        for n, x in enumerate(outs):
            first_at = at + sum(STACKS[:n])
            far_stacks.append((odd[first_at : first_at + STACKS[n]], x))
    for at in range(0, len(even), size):
        labels = even[at : at + size]
        kept.update(zip(labels, triangle(labels, other_near, F32, (1,) * size, after(meta, far_stacks[-1][1]))))
    gate = pl.pallas_call(
        gate_kernel,
        in_specs=[vmem] * 3,
        out_specs=vmem,
        out_shape=jax.ShapeDtypeStruct((band, rows, width), F32),
        compiler_params=pltpu.CompilerParams(vmem_limit_bytes=10 << 20),
        cost_estimate=pl.CostEstimate(flops=10**9, bytes_accessed=2 * 10**6, transcendentals=0),
        name="gate",
    )(own_band, w_gate, after(row_mask, kept[0]))

    arrived = {v: [(kept[v], 0)] for v in even}

    def send_far(n, *earlier):
        labels, x = far_stacks[n]
        for y in earlier:
            x = after(x, y)
        moved = swap(x, 1)
        for m, label in enumerate(labels):
            arrived[label - 1].append((moved, m * band))
        return moved

    def total(v):
        return sum(piece[start : start + band].astype(F32) for piece, start in arrived[v]).astype(BF16)

    def send(v, x=None):
        x = total(v) if x is None else x
        bit = v & -v
        moved = swap(x, bit)
        arrived[v - bit].append((moved, 0))
        return moved

    send_far(0)
    moved = send(even[0])
    for n in range(1, len(far_stacks)):
        send_far(n, kept[0] if n == 1 else moved)
    for v in even[1:-1]:
        send(v)
    pieces, starts = zip(*arrived[0])
    return pl.pallas_call(
        functools.partial(final_kernel, starts),
        in_specs=[vmem] * (len(pieces) + 3),
        out_specs=vmem,
        out_shape=jax.ShapeDtypeStruct((rows, band, width), BF16),
        scratch_shapes=[pltpu.VMEM((rows * (band + 8), width), F32)],
        compiler_params=pltpu.CompilerParams(vmem_limit_bytes=14 << 20),
        cost_estimate=pl.CostEstimate(flops=10**9, bytes_accessed=3 * 10**6, transcendentals=0),
        name="final",
    )(*pieces, gate, gain_o, w_out)


def solution(mesh):
    in_specs = (
        P(("grp", "ax", "nr"), None, None),
        P("grp"),
        P("grp"),
        P("grp"),
        P(),
        P(),
        P(),
        P(None, "nr"),
        P(None, "nr"),
        P(None, "nr"),
        P(None, "nr"),
    )
    out_specs = P(("grp", "ax", "nr"), None, None)
    return jax.shard_map(body, mesh=mesh, in_specs=in_specs, out_specs=out_specs, check_vma=False)
```

```python
import functools

import jax
import jax.numpy as jnp
from jax import lax
from jax.experimental import pallas as pl
from jax.experimental.pallas import tpu as pltpu
from jax.sharding import PartitionSpec as P

BAND = 48
NORM_EPS = 1e-05
GROUP = 4
F32, BF16, I32 = jnp.float32, jnp.bfloat16, jnp.int32
LAST = (((1,), (1,)), ((), ()))


def layer_norm(values, gain):
    mean = jnp.mean(values, -1, keepdims=True)
    centered = values - mean
    var = jnp.mean(centered * centered, -1, keepdims=True)
    return centered * lax.rsqrt(var + NORM_EPS) * gain


def place_of(label, ax, nr):
    swapped = (label & ~3) | ((label & 1) << 1) | ((label >> 1) & 1)
    return ax ^ (label + (swapped - label) * nr)


def pack_kernel(far_labels, near_labels, meta, pairs, weights, first, far, near, sems):
    window = first.shape[1] - 16
    ax, other = meta[0], 1 - meta[1]
    base = pl.multiple_of(meta[5], 16)
    copies = [pltpu.make_async_copy(pairs.at[:, pl.ds(base, window), :], first.at[:, 0:window, :], sems.at[0])]
    size = far.shape[2]
    for part, labels in ((far, far_labels), (near, near_labels)):
        for m, label in enumerate(labels):
            block = place_of(label, ax, other) * 2 + other
            rows = pl.ds(pl.multiple_of(block * size, size), size)
            copies.append(pltpu.make_async_copy(pairs.at[:, rows, :], part.at[:, m], sems.at[len(copies)]))
    for copy in copies:
        copy.start()
    half = weights.shape[0] // 3
    turned = [weights[n * half : (n + 1) * half].astype(F32).T.astype(BF16) for n in range(2)] + [weights[2 * half :]]
    turned = jnp.concatenate(turned + turned[:1], 0)
    for row in range(first.shape[0]):
        first[row, window:, :] = turned[row * 16 : row * 16 + 16]
    for copy in copies:
        copy.wait()


def right_kernel(
    chain_s, mask_s, meta, own, other, chain_cols, embed, gain, right_ref, w_left_ref, w_gate_ref, w_out_ref, band_ref,
    normed_scr, right_scr,
):
    rows, window, width = own.shape
    window -= 16
    band = BAND
    both = 2 * rows
    pitch, turn = window + 8, band + 8
    base = pl.multiple_of(meta[5], 16)
    offset = meta[4] - meta[5]
    first = meta[1] == 0
    chains = chain_cols[pl.ds(base, window), :]
    emb, gn = embed[...], gain[...]
    w_own = own[:, window:, :].reshape(rows * 16, width)
    w_other = other[:, window:, :].reshape(rows * 16, width)
    low, high = jnp.where(first, w_own, w_other), jnp.where(first, w_other, w_own)

    def weight(start, size):
        return jnp.concatenate([low[start : start + size], high[start : start + size]], 0)

    w_left_ref[...] = weight(0, width)
    w_right = weight(width, width)
    w_gate_ref[...] = weight(2 * width, width // 2)
    w_out_ref[...] = weight(2 * width + width // 2, width // 2)
    for source, start, ref in ((0, meta[2], own), (1, meta[3], other)):
        for k in range(rows):
            same = chains == chain_s[start + k]
            shifted = ref[k, 0:window].astype(F32) + jnp.where(same, emb, 0.0)
            keep = mask_s[start + k].astype(F32)
            row = (source * rows + k) * pitch
            normed_scr[row : row + window, :] = layer_norm(shifted, gn * keep)
    channel = lax.broadcasted_iota(I32, (width, 2 * both), 0)
    lane = lax.broadcasted_iota(I32, (width, 2 * both), 1)
    spread = ((channel & 1) == lane // both).astype(F32)
    for j in range(0, band, 2):
        normed = [normed_scr[pl.ds(offset + j + u, both, stride=pitch), :].astype(BF16) for u in range(2)]
        doubled = jnp.concatenate([normed[0], normed[0], normed[1], normed[1]], 0)
        proj = lax.dot_general(w_right, doubled, LAST, preferred_element_type=F32)
        edge = jax.nn.sigmoid(proj[:width]) * proj[width:]
        for u in range(2):
            keep = spread * mask_s[meta[4] + j + u].astype(F32)
            right_scr[pl.ds(j + u, width, stride=turn), :] = edge[:, u * 2 * both : (u + 1) * 2 * both] * keep
            band_ref[j + u] = normed[u][0:rows]
    for g in range(width // 2):
        pair = [right_scr[(2 * g + u) * turn : (2 * g + u) * turn + band, :] for u in range(2)]
        right_ref[g] = jnp.concatenate(pair, 0).astype(BF16)


def gate_kernel(band_ref, w_gate, mask_i, gate_ref):
    band, rows, width = band_ref.shape
    gate = lax.dot_general(band_ref[...].reshape(band * rows, width), w_gate[...], LAST, preferred_element_type=F32)
    gate_ref[...] = jax.nn.sigmoid(gate).reshape(band, rows, width) * mask_i[...][None]


def triangle_kernel(group, tile, stacks, out_type, chain_s, mask_s, meta, *refs):
    own = refs[:group]
    other = refs[group : 2 * group]
    chain_cols = refs[2 * group : 3 * group]
    embed, gain, w_left_ref, right_ref = refs[3 * group : 3 * group + 4]
    outs = refs[3 * group + 4 : -2]
    slots = [(n, m) for n, stack in enumerate(stacks) for m in range(stack)]
    left_scr, tri_scr = refs[-2:]
    pairs, band2, both2 = right_ref.shape
    width, band, both = pairs * 2, band2 // 2, both2 // 2
    rows = both // 2
    pitch, turn = both + 8, band + 8
    size = own[0].shape[2]
    lanes = group * size
    step = pl.program_id(0)
    w_left = w_left_ref[...]
    chains = jnp.concatenate([ref[...] for ref in chain_cols], 0)
    emb, gn = embed[...], gain[...]

    def normed(source, k):
        base = meta[3] if source else meta[2]
        values = jnp.concatenate([ref[k, 0] for ref in (other if source else own)], 0)
        same = chains == chain_s[base + step * tile + k]
        return layer_norm(values.astype(F32) + jnp.where(same, emb, 0.0), gn).astype(BF16)

    wide = 2 * width // (2 * lanes)
    for k in range(0, tile, wide):
        several = jnp.concatenate([normed(source, k + m) for source in range(2) for m in range(wide)], 0)
        proj = lax.dot_general(w_left, several, LAST, preferred_element_type=F32)
        edge = jax.nn.sigmoid(proj[:width]) * proj[width:]
        for n in range(2 * wide):
            at = step * tile + k + n // wide * rows + n % wide
            left_scr[pl.ds(at, width, stride=pitch), :] = edge[:, n * lanes : (n + 1) * lanes]

    @pl.when(step == pl.num_programs(0) - 1)
    def _():
        for g in range(pairs):
            left = jnp.concatenate([left_scr[c * pitch : c * pitch + both, :] for c in (2 * g, 2 * g + 1)], 0)
            tri = jnp.dot(right_ref[g], left.astype(BF16), preferred_element_type=F32)
            tri_scr[2 * g * turn : 2 * g * turn + band, :] = tri[:band]
            tri_scr[(2 * g + 1) * turn : (2 * g + 1) * turn + band, :] = tri[band:]
        for j in range(band):
            turned = tri_scr[pl.ds(j, width, stride=turn), :].T
            for b in range(group):
                outs[slots[b][0]][slots[b][1] * band + j] = turned[b * size : (b + 1) * size].astype(out_type)


def final_kernel(starts, *refs):
    pieces = refs[: len(starts)]
    gate_ref, gain, w_out, out_ref, scr = refs[len(starts) :]
    band, rows, width = gate_ref.shape
    turn = band + 8
    total = pieces[0][...]
    for ref, start in zip(pieces[1:], starts[1:]):
        total = total + ref[start : start + band].astype(F32)
    normed = layer_norm(total.reshape(band * rows, width), gain[...]).astype(BF16)
    projected = lax.dot_general(normed, w_out[...], LAST, preferred_element_type=F32)
    for j in range(band):
        scr[pl.ds(j, rows, stride=turn), :] = projected[j * rows : (j + 1) * rows] * gate_ref[j]
    for i in range(rows):
        out_ref[i] = scr[i * turn : i * turn + band, :].astype(BF16)


def body(pair_map, chain_ids, token_mask, band_start, chain_embed, gain_in, gain_out, w_left, w_right, w_gate, w_out):
    rows, tokens, width = pair_map.shape
    n_ax = lax.axis_size("ax")
    ax, nr = lax.axis_index("ax"), lax.axis_index("nr")
    band, tile = BAND, 8
    odd, even = list(range(n_ax - 1, 0, -2)), list(range(n_ax - 2, -1, -2))
    both = 2 * rows
    window = band + 16
    vmem = pl.BlockSpec(memory_space=pltpu.VMEM)
    smem = pl.BlockSpec(memory_space=pltpu.SMEM)
    hbm = pl.BlockSpec(memory_space=pltpu.HBM)

    def swap_core(x):
        return lax.ppermute(x, "nr", [(0, 1), (1, 0)])

    def swap(x, bit):
        pairs = []
        for s in range(n_ax):
            for core in range(2):
                pairs.append((s * 2 + core, place_of(bit, s, core) * 2 + core))
        return lax.ppermute(x, ("ax", "nr"), pairs)

    def after(x, done):
        return lax.optimization_barrier((x, done))[0]

    start = band_start[0]
    own_row, other_row = (ax * 2 + nr) * rows, (ax * 2 + 1 - nr) * rows
    meta = jnp.stack([ax, nr, own_row, other_row, start, jnp.minimum(start // 16 * 16, tokens - window)]).astype(I32)

    part_shape = jax.ShapeDtypeStruct((rows, n_ax // 2, rows, width), BF16)
    weights = jnp.concatenate([w_left, w_right, w_gate.T, w_out.T], 0)
    own_first, far, near = pl.pallas_call(
        functools.partial(pack_kernel, odd, even),
        in_specs=[smem, hbm, vmem],
        out_specs=[vmem] * 3,
        out_shape=[jax.ShapeDtypeStruct((rows, window + 16, width), BF16), part_shape, part_shape],
        scratch_shapes=[pltpu.SemaphoreType.DMA((1 + n_ax,))],
        compiler_params=pltpu.CompilerParams(vmem_limit_bytes=10 << 20),
        name="pack",
    )(meta, pair_map, weights)
    other_first = swap_core(own_first)
    other_far = swap_core(after(far, other_first))
    own_blocks = pair_map.reshape(rows, tokens // rows, rows, width)
    chain_cols = jnp.broadcast_to(chain_ids[:, None], (tokens, 128))
    row_mask = jnp.broadcast_to(
        lax.dynamic_slice_in_dim(token_mask, own_row, rows).astype(F32)[:, None], (rows, width)
    )
    embed, gain, gain_o = chain_embed[None], gain_in[None], gain_out[None]

    right, w_left, w_gate, w_out, own_band = pl.pallas_call(
        right_kernel,
        grid_spec=pltpu.PrefetchScalarGridSpec(
            num_scalar_prefetch=3,
            grid=(),
            in_specs=[vmem] * 5,
            out_specs=[vmem] * 5,
            scratch_shapes=[
                pltpu.VMEM((both * (window + 8), width), F32),
                pltpu.VMEM((width * (band + 8), 2 * both), F32),
            ],
        ),
        out_shape=[
            jax.ShapeDtypeStruct((width // 2, 2 * band, 2 * both), BF16),
            jax.ShapeDtypeStruct((2 * width, width), BF16),
            jax.ShapeDtypeStruct((width, width), BF16),
            jax.ShapeDtypeStruct((width, width), BF16),
            jax.ShapeDtypeStruct((band, rows, width), BF16),
        ],
        compiler_params=pltpu.CompilerParams(vmem_limit_bytes=18 << 20),
        cost_estimate=pl.CostEstimate(flops=4 * 10**9, bytes_accessed=2 * 10**6, transcendentals=0),
        name="right",
    )(chain_ids, token_mask, meta, own_first, other_first, chain_cols, embed, gain)

    other_near = swap_core(after(near, right))

    def triangle(labels, other_part, out_type, stacks, scalars):
        group = len(labels)
        row_specs, part_specs, chain_specs = [], [], []
        for v in labels:
            row_specs.append(
                pl.BlockSpec(
                    (tile, 1, rows, width),
                    lambda t, c, m, meta, v=v: (t, place_of(v, meta[0], meta[1]) * 2 + meta[1], 0, 0),
                )
            )
            at = (odd if v & 1 else even).index(v)
            part_specs.append(pl.BlockSpec((tile, 1, rows, width), lambda t, c, m, meta, at=at: (t, at, 0, 0)))
            chain_specs.append(
                pl.BlockSpec((rows, 128), lambda t, c, m, meta, v=v: (place_of(v, meta[0], meta[1]) * 2 + meta[1], 0))
            )
        whole = lambda shape: pl.BlockSpec(shape, lambda t, c, m, meta: (0,) * len(shape))
        out_shapes = [(stack * band, rows, width) for stack in stacks]
        return pl.pallas_call(
            functools.partial(triangle_kernel, group, tile, stacks, out_type),
            grid_spec=pltpu.PrefetchScalarGridSpec(
                num_scalar_prefetch=3,
                grid=(rows // tile,),
                in_specs=row_specs
                + part_specs
                + chain_specs
                + [whole((1, width)), whole((1, width)), whole(w_left.shape), whole(right.shape)],
                out_specs=[whole(shape) for shape in out_shapes],
                scratch_shapes=[
                    pltpu.VMEM((width * (both + 8), group * rows), F32),
                    pltpu.VMEM((width * (band + 8), group * rows), F32),
                ],
            ),
            out_shape=[jax.ShapeDtypeStruct(shape, out_type) for shape in out_shapes],
            compiler_params=pltpu.CompilerParams(vmem_limit_bytes=28 << 20),
            cost_estimate=pl.CostEstimate(flops=8 * 10**9, bytes_accessed=4 * 10**6, transcendentals=0),
            name="triangle",
        )(
            chain_ids, token_mask, scalars, *([own_blocks] * group), *([other_part] * group), *([chain_cols] * group),
            embed, gain, w_left, right,
        )

    size = GROUP
    far_stacks, kept = [], {}

    def far_call(at, stacks, scalars):
        labels = odd[at : at + sum(stacks)]
        for x in triangle(labels, other_far, BF16, stacks, scalars):
            count = x.shape[0] // band
            far_stacks.append((labels[:count], x))
            labels = labels[count:]

    far_call(0, (2,), meta)
    last = far_stacks[-1][1]
    for at in range(0, len(even), size):
        labels = even[at : at + size]
        kept.update(zip(labels, triangle(labels, other_near, F32, (1,) * size, after(meta, last))))
        last = kept[labels[-1]]
    gate = pl.pallas_call(
        gate_kernel,
        in_specs=[vmem] * 3,
        out_specs=vmem,
        out_shape=jax.ShapeDtypeStruct((band, rows, width), F32),
        compiler_params=pltpu.CompilerParams(vmem_limit_bytes=10 << 20),
        cost_estimate=pl.CostEstimate(flops=10**9, bytes_accessed=2 * 10**6, transcendentals=0),
        name="gate",
    )(own_band, w_gate, after(row_mask, kept[0]))

    arrived = {v: [(kept[v], 0)] for v in even}

    def send_far(n, *earlier):
        labels, x = far_stacks[n]
        for y in earlier:
            x = after(x, y)
        moved = swap(x, 1)
        for m, label in enumerate(labels):
            arrived[label - 1].append((moved, m * band))
        return moved

    def total(v):
        return sum(piece[start : start + band].astype(F32) for piece, start in arrived[v]).astype(BF16)

    def send(v, x=None):
        x = total(v) if x is None else x
        bit = v & -v
        moved = swap(x, bit)
        arrived[v - bit].append((moved, 0))
        return moved

    send_far(0)
    x = total(even[0])
    moved = send(even[0], x)
    for at in range(2, len(odd), 2):
        far_call(at, (1, 1), after(meta, x))
        x = far_stacks[-1][1]
    for n in range(1, len(far_stacks)):
        send_far(n)
    for v in even[1:-1]:
        send(v)

    pieces, starts = zip(*arrived[0])
    return pl.pallas_call(
        functools.partial(final_kernel, starts),
        in_specs=[vmem] * (len(pieces) + 3),
        out_specs=vmem,
        out_shape=jax.ShapeDtypeStruct((rows, band, width), BF16),
        scratch_shapes=[pltpu.VMEM((rows * (band + 8), width), F32)],
        compiler_params=pltpu.CompilerParams(vmem_limit_bytes=14 << 20),
        cost_estimate=pl.CostEstimate(flops=10**9, bytes_accessed=3 * 10**6, transcendentals=0),
        name="final",
    )(*pieces, gate, gain_o, w_out)


def solution(mesh):
    in_specs = (
        P(("grp", "ax", "nr"), None, None),
        P("grp"),
        P("grp"),
        P("grp"),
        P(),
        P(),
        P(),
        P(None, "nr"),
        P(None, "nr"),
        P(None, "nr"),
        P(None, "nr"),
    )
    out_specs = P(("grp", "ax", "nr"), None, None)
    return jax.shard_map(body, mesh=mesh, in_specs=in_specs, out_specs=out_specs, check_vma=False)
```

```python
import functools

import jax
import jax.numpy as jnp
from jax import lax
from jax.experimental import pallas as pl
from jax.experimental.pallas import tpu as pltpu
from jax.sharding import PartitionSpec as P

BAND = 48
NORM_EPS = 1e-05
GROUP = 4
F32, BF16, I32 = jnp.float32, jnp.bfloat16, jnp.int32
LAST = (((1,), (1,)), ((), ()))


def layer_norm(values, gain):
    mean = jnp.mean(values, -1, keepdims=True)
    centered = values - mean
    var = jnp.mean(centered * centered, -1, keepdims=True)
    return centered * lax.rsqrt(var + NORM_EPS) * gain


def place_of(label, ax, nr):
    swapped = (label & ~3) | ((label & 1) << 1) | ((label >> 1) & 1)
    return ax ^ (label + (swapped - label) * nr)


def pack_kernel(far_labels, near_labels, meta, pairs, first, far, near, sems):
    window = first.shape[1]
    ax, other = meta[0], 1 - meta[1]
    base = pl.multiple_of(meta[5], 16)
    copies = [pltpu.make_async_copy(pairs.at[:, pl.ds(base, window), :], first, sems.at[0])]
    size = far.shape[2]
    for part, labels in ((far, far_labels), (near, near_labels)):
        for m, label in enumerate(labels):
            block = place_of(label, ax, other) * 2 + other
            rows = pl.ds(pl.multiple_of(block * size, size), size)
            copies.append(pltpu.make_async_copy(pairs.at[:, rows, :], part.at[:, m], sems.at[len(copies)]))
    for copy in copies:
        copy.start()
    for copy in copies:
        copy.wait()


def right_kernel(
    chain_s, mask_s, meta, own, other, own_weights, other_weights, chain_cols, embed, gain, right_ref, w_left_ref, w_gate_ref, w_out_ref, band_ref,
    normed_scr, right_scr,
):
    rows, window, width = own.shape
    band = BAND
    both = 2 * rows
    pitch, turn = window + 8, band + 8
    base = pl.multiple_of(meta[5], 16)
    offset = meta[4] - meta[5]
    first = meta[1] == 0
    chains = chain_cols[pl.ds(base, window), :]
    emb, gn = embed[...], gain[...]
    half = own_weights.shape[0] // 3

    def rows_first(ref):
        turned = [ref[n * half : (n + 1) * half].astype(F32).T.astype(BF16) for n in range(2)]
        return jnp.concatenate(turned + [ref[2 * half :]], 0)

    w_own, w_other = rows_first(own_weights), rows_first(other_weights)
    low, high = jnp.where(first, w_own, w_other), jnp.where(first, w_other, w_own)

    def weight(start, size):
        return jnp.concatenate([low[start : start + size], high[start : start + size]], 0)

    w_left_ref[...] = weight(0, width)
    w_right = weight(width, width)
    w_gate_ref[...] = weight(2 * width, width // 2)
    w_out_ref[...] = weight(2 * width + width // 2, width // 2)
    for source, start, ref in ((0, meta[2], own), (1, meta[3], other)):
        for k in range(rows):
            same = chains == chain_s[start + k]
            shifted = ref[k, 0:window].astype(F32) + jnp.where(same, emb, 0.0)
            keep = mask_s[start + k].astype(F32)
            row = (source * rows + k) * pitch
            normed_scr[row : row + window, :] = layer_norm(shifted, gn * keep)
    channel = lax.broadcasted_iota(I32, (width, 2 * both), 0)
    lane = lax.broadcasted_iota(I32, (width, 2 * both), 1)
    spread = ((channel & 1) == lane // both).astype(F32)
    for j in range(0, band, 2):
        normed = [normed_scr[pl.ds(offset + j + u, both, stride=pitch), :].astype(BF16) for u in range(2)]
        doubled = jnp.concatenate([normed[0], normed[0], normed[1], normed[1]], 0)
        proj = lax.dot_general(w_right, doubled, LAST, preferred_element_type=F32)
        edge = jax.nn.sigmoid(proj[:width]) * proj[width:]
        for u in range(2):
            keep = spread * mask_s[meta[4] + j + u].astype(F32)
            right_scr[pl.ds(j + u, width, stride=turn), :] = edge[:, u * 2 * both : (u + 1) * 2 * both] * keep
            band_ref[j + u] = normed[u][0:rows]
    for g in range(width // 2):
        pair = [right_scr[(2 * g + u) * turn : (2 * g + u) * turn + band, :] for u in range(2)]
        right_ref[g] = jnp.concatenate(pair, 0).astype(BF16)


def gate_kernel(band_ref, w_gate, mask_i, gate_ref):
    band, rows, width = band_ref.shape
    gate = lax.dot_general(band_ref[...].reshape(band * rows, width), w_gate[...], LAST, preferred_element_type=F32)
    gate_ref[...] = jax.nn.sigmoid(gate).reshape(band, rows, width) * mask_i[...][None]


def triangle_kernel(group, tile, stacks, out_type, chain_s, mask_s, meta, *refs):
    own = refs[:group]
    other = refs[group : 2 * group]
    chain_cols = refs[2 * group : 3 * group]
    embed, gain, w_left_ref, right_ref = refs[3 * group : 3 * group + 4]
    outs = refs[3 * group + 4 : -2]
    slots = [(n, m) for n, stack in enumerate(stacks) for m in range(stack)]
    left_scr, tri_scr = refs[-2:]
    pairs, band2, both2 = right_ref.shape
    width, band, both = pairs * 2, band2 // 2, both2 // 2
    rows = both // 2
    pitch, turn = both + 8, band + 8
    size = own[0].shape[2]
    lanes = group * size
    step = pl.program_id(0)
    w_left = w_left_ref[...]
    chains = jnp.concatenate([ref[...] for ref in chain_cols], 0)
    emb, gn = embed[...], gain[...]

    def normed(source, k):
        base = meta[3] if source else meta[2]
        values = jnp.concatenate([ref[k, 0] for ref in (other if source else own)], 0)
        same = chains == chain_s[base + step * tile + k]
        return layer_norm(values.astype(F32) + jnp.where(same, emb, 0.0), gn).astype(BF16)

    wide = 2 * width // (2 * lanes)
    for k in range(0, tile, wide):
        several = jnp.concatenate([normed(source, k + m) for source in range(2) for m in range(wide)], 0)
        proj = lax.dot_general(w_left, several, LAST, preferred_element_type=F32)
        edge = jax.nn.sigmoid(proj[:width]) * proj[width:]
        for n in range(2 * wide):
            at = step * tile + k + n // wide * rows + n % wide
            left_scr[pl.ds(at, width, stride=pitch), :] = edge[:, n * lanes : (n + 1) * lanes]

    @pl.when(step == pl.num_programs(0) - 1)
    def _():
        for g in range(pairs):
            left = jnp.concatenate([left_scr[c * pitch : c * pitch + both, :] for c in (2 * g, 2 * g + 1)], 0)
            tri = jnp.dot(right_ref[g], left.astype(BF16), preferred_element_type=F32)
            tri_scr[2 * g * turn : 2 * g * turn + band, :] = tri[:band]
            tri_scr[(2 * g + 1) * turn : (2 * g + 1) * turn + band, :] = tri[band:]
        for j in range(band):
            turned = tri_scr[pl.ds(j, width, stride=turn), :].T
            for b in range(group):
                outs[slots[b][0]][slots[b][1] * band + j] = turned[b * size : (b + 1) * size].astype(out_type)


def merge_kernel(starts, *refs):
    out = refs[-1]
    total = refs[0][...]
    for ref, start in zip(refs[1:-1], starts[1:]):
        total = total + ref[start : start + out.shape[0]].astype(F32)
    out[...] = total.astype(BF16)


def final_kernel(starts, *refs):
    pieces = refs[: len(starts)]
    gate_ref, gain, w_out, out_ref, scr = refs[len(starts) :]
    band, rows, width = gate_ref.shape
    turn = band + 8
    total = pieces[0][...]
    for ref, start in zip(pieces[1:], starts[1:]):
        total = total + ref[start : start + band].astype(F32)
    normed = layer_norm(total.reshape(band * rows, width), gain[...]).astype(BF16)
    projected = lax.dot_general(normed, w_out[...], LAST, preferred_element_type=F32)
    for j in range(band):
        scr[pl.ds(j, rows, stride=turn), :] = projected[j * rows : (j + 1) * rows] * gate_ref[j]
    for i in range(rows):
        out_ref[i] = scr[i * turn : i * turn + band, :].astype(BF16)


def body(pair_map, chain_ids, token_mask, band_start, chain_embed, gain_in, gain_out, w_left, w_right, w_gate, w_out):
    rows, tokens, width = pair_map.shape
    n_ax = lax.axis_size("ax")
    ax, nr = lax.axis_index("ax"), lax.axis_index("nr")
    band, tile = BAND, 8
    odd, even = list(range(n_ax - 1, 0, -2)), list(range(n_ax - 2, -1, -2))
    both = 2 * rows
    window = band + 16
    vmem = pl.BlockSpec(memory_space=pltpu.VMEM)
    smem = pl.BlockSpec(memory_space=pltpu.SMEM)
    hbm = pl.BlockSpec(memory_space=pltpu.HBM)

    def swap_core(x):
        return lax.ppermute(x, "nr", [(0, 1), (1, 0)])

    def swap(x, bit):
        pairs = []
        for s in range(n_ax):
            for core in range(2):
                pairs.append((s * 2 + core, place_of(bit, s, core) * 2 + core))
        return lax.ppermute(x, ("ax", "nr"), pairs)

    def after(x, done):
        return lax.optimization_barrier((x, done))[0]

    start = band_start[0]
    own_row, other_row = (ax * 2 + nr) * rows, (ax * 2 + 1 - nr) * rows
    meta = jnp.stack([ax, nr, own_row, other_row, start, jnp.minimum(start // 16 * 16, tokens - window)]).astype(I32)

    part_shape = jax.ShapeDtypeStruct((rows, n_ax // 2, rows, width), BF16)
    weights = jnp.concatenate([w_left, w_right, w_gate.T, w_out.T], 0)
    own_first, far, near = pl.pallas_call(
        functools.partial(pack_kernel, odd, even),
        in_specs=[smem, hbm],
        out_specs=[vmem] * 3,
        out_shape=[jax.ShapeDtypeStruct((rows, window, width), BF16), part_shape, part_shape],
        scratch_shapes=[pltpu.SemaphoreType.DMA((1 + n_ax,))],
        compiler_params=pltpu.CompilerParams(vmem_limit_bytes=10 << 20),
        name="pack",
    )(meta, pair_map)
    other_weights = swap_core(weights)
    other_first = swap_core(own_first)
    other_far = swap_core(lax.optimization_barrier((far, other_first, other_weights))[0])
    own_blocks = pair_map.reshape(rows, tokens // rows, rows, width)
    chain_cols = jnp.broadcast_to(chain_ids[:, None], (tokens, 128))
    row_mask = jnp.broadcast_to(
        lax.dynamic_slice_in_dim(token_mask, own_row, rows).astype(F32)[:, None], (rows, width)
    )
    embed, gain, gain_o = chain_embed[None], gain_in[None], gain_out[None]

    right, w_left, w_gate, w_out, own_band = pl.pallas_call(
        right_kernel,
        grid_spec=pltpu.PrefetchScalarGridSpec(
            num_scalar_prefetch=3,
            grid=(),
            in_specs=[vmem] * 7,
            out_specs=[vmem] * 5,
            scratch_shapes=[
                pltpu.VMEM((both * (window + 8), width), F32),
                pltpu.VMEM((width * (band + 8), 2 * both), F32),
            ],
        ),
        out_shape=[
            jax.ShapeDtypeStruct((width // 2, 2 * band, 2 * both), BF16),
            jax.ShapeDtypeStruct((2 * width, width), BF16),
            jax.ShapeDtypeStruct((width, width), BF16),
            jax.ShapeDtypeStruct((width, width), BF16),
            jax.ShapeDtypeStruct((band, rows, width), BF16),
        ],
        compiler_params=pltpu.CompilerParams(vmem_limit_bytes=18 << 20),
        cost_estimate=pl.CostEstimate(flops=4 * 10**9, bytes_accessed=2 * 10**6, transcendentals=0),
        name="right",
    )(chain_ids, token_mask, meta, own_first, other_first, weights, other_weights, chain_cols, embed, gain)

    other_near = swap_core(after(near, right))

    def triangle(labels, other_part, out_type, stacks, scalars):
        group = len(labels)
        row_specs, part_specs, chain_specs = [], [], []
        for v in labels:
            row_specs.append(
                pl.BlockSpec(
                    (tile, 1, rows, width),
                    lambda t, c, m, meta, v=v: (t, place_of(v, meta[0], meta[1]) * 2 + meta[1], 0, 0),
                )
            )
            at = (odd if v & 1 else even).index(v)
            part_specs.append(pl.BlockSpec((tile, 1, rows, width), lambda t, c, m, meta, at=at: (t, at, 0, 0)))
            chain_specs.append(
                pl.BlockSpec((rows, 128), lambda t, c, m, meta, v=v: (place_of(v, meta[0], meta[1]) * 2 + meta[1], 0))
            )
        whole = lambda shape: pl.BlockSpec(shape, lambda t, c, m, meta: (0,) * len(shape))
        out_shapes = [(stack * band, rows, width) for stack in stacks]
        return pl.pallas_call(
            functools.partial(triangle_kernel, group, tile, stacks, out_type),
            grid_spec=pltpu.PrefetchScalarGridSpec(
                num_scalar_prefetch=3,
                grid=(rows // tile,),
                in_specs=row_specs
                + part_specs
                + chain_specs
                + [whole((1, width)), whole((1, width)), whole(w_left.shape), whole(right.shape)],
                out_specs=[whole(shape) for shape in out_shapes],
                scratch_shapes=[
                    pltpu.VMEM((width * (both + 8), group * rows), F32),
                    pltpu.VMEM((width * (band + 8), group * rows), F32),
                ],
            ),
            out_shape=[jax.ShapeDtypeStruct(shape, out_type) for shape in out_shapes],
            compiler_params=pltpu.CompilerParams(vmem_limit_bytes=28 << 20),
            cost_estimate=pl.CostEstimate(flops=8 * 10**9, bytes_accessed=4 * 10**6, transcendentals=0),
            name="triangle",
        )(
            chain_ids, token_mask, scalars, *([own_blocks] * group), *([other_part] * group), *([chain_cols] * group),
            embed, gain, w_left, right,
        )

    size = GROUP
    far_stacks, kept = [], {}

    def far_call(at, stacks, scalars):
        labels = odd[at : at + sum(stacks)]
        for x in triangle(labels, other_far, BF16, stacks, scalars):
            count = x.shape[0] // band
            far_stacks.append((labels[:count], x))
            labels = labels[count:]

    far_call(0, (2,), meta)
    last = far_stacks[-1][1]
    for at in range(0, len(even), size):
        labels = even[at : at + size]
        kept.update(zip(labels, triangle(labels, other_near, F32, (1,) * size, after(meta, last))))
        last = kept[labels[-1]]
    gate = pl.pallas_call(
        gate_kernel,
        in_specs=[vmem] * 3,
        out_specs=vmem,
        out_shape=jax.ShapeDtypeStruct((band, rows, width), F32),
        compiler_params=pltpu.CompilerParams(vmem_limit_bytes=10 << 20),
        cost_estimate=pl.CostEstimate(flops=10**9, bytes_accessed=2 * 10**6, transcendentals=0),
        name="gate",
    )(own_band, w_gate, after(row_mask, kept[0]))

    arrived = {v: [(kept[v], 0)] for v in even}

    def send_far(n, *earlier):
        labels, x = far_stacks[n]
        for y in earlier:
            x = after(x, y)
        moved = swap(x, 1)
        for m, label in enumerate(labels):
            arrived[label - 1].append((moved, m * band))
        return moved

    def total(v):
        if len(arrived[v]) > 2:
            parts, offsets = zip(*arrived[v])
            return pl.pallas_call(
                functools.partial(merge_kernel, offsets),
                in_specs=[vmem] * len(parts),
                out_specs=vmem,
                out_shape=jax.ShapeDtypeStruct((band, rows, width), BF16),
                compiler_params=pltpu.CompilerParams(vmem_limit_bytes=8 << 20),
                cost_estimate=pl.CostEstimate(flops=10**6, bytes_accessed=10**5, transcendentals=0),
                name="merge",
            )(*parts)
        return sum(piece[start : start + band].astype(F32) for piece, start in arrived[v]).astype(BF16)

    def send(v, x=None):
        x = total(v) if x is None else x
        bit = v & -v
        moved = swap(x, bit)
        arrived[v - bit].append((moved, 0))
        return moved

    send_far(0)
    x = total(even[0])
    moved = send(even[0], x)
    for at in range(2, len(odd), 2):
        far_call(at, (1, 1), after(meta, x))
        x = far_stacks[-1][1]
    for n in range(1, len(far_stacks)):
        send_far(n)
    for v in even[1:-1]:
        send(v)

    pieces, starts = zip(*arrived[0])
    return pl.pallas_call(
        functools.partial(final_kernel, starts),
        in_specs=[vmem] * (len(pieces) + 3),
        out_specs=vmem,
        out_shape=jax.ShapeDtypeStruct((rows, band, width), BF16),
        scratch_shapes=[pltpu.VMEM((rows * (band + 8), width), F32)],
        compiler_params=pltpu.CompilerParams(vmem_limit_bytes=14 << 20),
        cost_estimate=pl.CostEstimate(flops=10**9, bytes_accessed=3 * 10**6, transcendentals=0),
        name="final",
    )(*pieces, gate, gain_o, w_out)


def solution(mesh):
    in_specs = (
        P(("grp", "ax", "nr"), None, None),
        P("grp"),
        P("grp"),
        P("grp"),
        P(),
        P(),
        P(),
        P(None, "nr"),
        P(None, "nr"),
        P(None, "nr"),
        P(None, "nr"),
    )
    out_specs = P(("grp", "ax", "nr"), None, None)
    return jax.shard_map(body, mesh=mesh, in_specs=in_specs, out_specs=out_specs, check_vma=False)
```

```python
import functools

import jax
import jax.numpy as jnp
from jax import lax
from jax.experimental import pallas as pl
from jax.experimental.pallas import tpu as pltpu
from jax.sharding import PartitionSpec as P

BAND = 48
NORM_EPS = 1e-05
GROUP = 4
F32, BF16, I32 = jnp.float32, jnp.bfloat16, jnp.int32
LAST = (((1,), (1,)), ((), ()))


def layer_norm(values, gain):
    mean = jnp.mean(values, -1, keepdims=True)
    centered = values - mean
    var = jnp.mean(centered * centered, -1, keepdims=True)
    return centered * lax.rsqrt(var + NORM_EPS) * gain


def place_of(label, ax, nr):
    swapped = (label & ~3) | ((label & 1) << 1) | ((label >> 1) & 1)
    return ax ^ (label + (swapped - label) * nr)


def pack_kernel(far_labels, near_labels, meta, pairs, first, far, near, sems):
    window = first.shape[1]
    ax, other = meta[0], 1 - meta[1]
    base = pl.multiple_of(meta[5], 16)
    copies = [pltpu.make_async_copy(pairs.at[:, pl.ds(base, window), :], first, sems.at[0])]
    size = far.shape[2]
    for part, labels in ((far, far_labels), (near, near_labels)):
        for m, label in enumerate(labels):
            block = place_of(label, ax, other) * 2 + other
            rows = pl.ds(pl.multiple_of(block * size, size), size)
            copies.append(pltpu.make_async_copy(pairs.at[:, rows, :], part.at[:, m], sems.at[len(copies)]))
    for copy in copies:
        copy.start()
    for copy in copies:
        copy.wait()


def right_kernel(
    chain_s, mask_s, meta, own, other, own_weights, other_weights, chain_cols, embed, gain, right_ref, w_left_ref, w_gate_ref, w_out_ref, band_ref,
    normed_scr, right_scr,
):
    rows, window, width = own.shape
    band = BAND
    both = 2 * rows
    pitch, turn = window + 8, band + 8
    base = pl.multiple_of(meta[5], 16)
    offset = meta[4] - meta[5]
    first = meta[1] == 0
    chains = chain_cols[pl.ds(base, window), :]
    emb, gn = embed[...], gain[...]
    half = own_weights.shape[0] // 3

    def rows_first(ref):
        turned = [ref[n * half : (n + 1) * half].astype(F32).T.astype(BF16) for n in range(2)]
        return jnp.concatenate(turned + [ref[2 * half :]], 0)

    w_own, w_other = rows_first(own_weights), rows_first(other_weights)
    low, high = jnp.where(first, w_own, w_other), jnp.where(first, w_other, w_own)

    def weight(start, size):
        return jnp.concatenate([low[start : start + size], high[start : start + size]], 0)

    w_left_ref[...] = weight(0, width)
    w_right = weight(width, width)
    w_gate_ref[...] = weight(2 * width, width // 2)
    w_out_ref[...] = weight(2 * width + width // 2, width // 2)
    for source, start, ref in ((0, meta[2], own), (1, meta[3], other)):
        for k in range(rows):
            same = chains == chain_s[start + k]
            shifted = ref[k, 0:window].astype(F32) + jnp.where(same, emb, 0.0)
            keep = mask_s[start + k].astype(F32)
            row = (source * rows + k) * pitch
            normed_scr[row : row + window, :] = layer_norm(shifted, gn * keep)
    channel = lax.broadcasted_iota(I32, (width, 2 * both), 0)
    lane = lax.broadcasted_iota(I32, (width, 2 * both), 1)
    spread = ((channel & 1) == lane // both).astype(F32)
    for j in range(0, band, 2):
        normed = [normed_scr[pl.ds(offset + j + u, both, stride=pitch), :].astype(BF16) for u in range(2)]
        doubled = jnp.concatenate([normed[0], normed[0], normed[1], normed[1]], 0)
        proj = lax.dot_general(w_right, doubled, LAST, preferred_element_type=F32)
        edge = jax.nn.sigmoid(proj[:width]) * proj[width:]
        for u in range(2):
            keep = spread * mask_s[meta[4] + j + u].astype(F32)
            right_scr[pl.ds(j + u, width, stride=turn), :] = edge[:, u * 2 * both : (u + 1) * 2 * both] * keep
            band_ref[j + u] = normed[u][0:rows]
    for g in range(width // 2):
        pair = [right_scr[(2 * g + u) * turn : (2 * g + u) * turn + band, :] for u in range(2)]
        right_ref[g] = jnp.concatenate(pair, 0).astype(BF16)


def gate_kernel(band_ref, w_gate, mask_i, gate_ref):
    band, rows, width = band_ref.shape
    gate = lax.dot_general(band_ref[...].reshape(band * rows, width), w_gate[...], LAST, preferred_element_type=F32)
    gate_ref[...] = jax.nn.sigmoid(gate).reshape(band, rows, width) * mask_i[...][None]


def triangle_kernel(group, tile, stacks, out_type, chain_s, mask_s, meta, *refs):
    own = refs[:group]
    other = refs[group : 2 * group]
    chain_cols = refs[2 * group : 3 * group]
    embed, gain, w_left_ref, right_ref = refs[3 * group : 3 * group + 4]
    outs = refs[3 * group + 4 : -2]
    slots = [(n, m) for n, stack in enumerate(stacks) for m in range(stack)]
    left_scr, tri_scr = refs[-2:]
    pairs, band2, both2 = right_ref.shape
    width, band, both = pairs * 2, band2 // 2, both2 // 2
    rows = both // 2
    pitch, turn = both + 8, band + 8
    size = own[0].shape[2]
    lanes = group * size
    step = pl.program_id(0)
    w_left = w_left_ref[...]
    chains = jnp.concatenate([ref[...] for ref in chain_cols], 0)
    emb, gn = embed[...], gain[...]

    def normed(source, k):
        base = meta[3] if source else meta[2]
        values = jnp.concatenate([ref[k, 0] for ref in (other if source else own)], 0)
        same = chains == chain_s[base + step * tile + k]
        return layer_norm(values.astype(F32) + jnp.where(same, emb, 0.0), gn).astype(BF16)

    wide = 2 * width // (2 * lanes)
    for k in range(0, tile, wide):
        several = jnp.concatenate([normed(source, k + m) for source in range(2) for m in range(wide)], 0)
        proj = lax.dot_general(w_left, several, LAST, preferred_element_type=F32)
        edge = jax.nn.sigmoid(proj[:width]) * proj[width:]
        for n in range(2 * wide):
            at = step * tile + k + n // wide * rows + n % wide
            left_scr[pl.ds(at, width, stride=pitch), :] = edge[:, n * lanes : (n + 1) * lanes]

    @pl.when(step == pl.num_programs(0) - 1)
    def _():
        for g in range(pairs):
            left = jnp.concatenate([left_scr[c * pitch : c * pitch + both, :] for c in (2 * g, 2 * g + 1)], 0)
            tri = jnp.dot(right_ref[g], left.astype(BF16), preferred_element_type=F32)
            tri_scr[2 * g * turn : 2 * g * turn + band, :] = tri[:band]
            tri_scr[(2 * g + 1) * turn : (2 * g + 1) * turn + band, :] = tri[band:]
        for j in range(band):
            turned = tri_scr[pl.ds(j, width, stride=turn), :].T
            for b in range(group):
                outs[slots[b][0]][slots[b][1] * band + j] = turned[b * size : (b + 1) * size].astype(out_type)


def merge_kernel(starts, *refs):
    out = refs[-1]
    total = refs[0][...]
    for ref, start in zip(refs[1:-1], starts[1:]):
        total = total + ref[start : start + out.shape[0]].astype(F32)
    out[...] = total.astype(BF16)


def final_kernel(starts, *refs):
    pieces = refs[: len(starts)]
    gate_ref, gain, w_out, out_ref, scr = refs[len(starts) :]
    band, rows, width = gate_ref.shape
    turn = band + 8
    total = pieces[0][...]
    for ref, start in zip(pieces[1:], starts[1:]):
        total = total + ref[start : start + band].astype(F32)
    normed = layer_norm(total.reshape(band * rows, width), gain[...]).astype(BF16)
    projected = lax.dot_general(normed, w_out[...], LAST, preferred_element_type=F32)
    for j in range(band):
        scr[pl.ds(j, rows, stride=turn), :] = projected[j * rows : (j + 1) * rows] * gate_ref[j]
    for i in range(rows):
        out_ref[i] = scr[i * turn : i * turn + band, :].astype(BF16)


def body(pair_map, chain_ids, token_mask, band_start, chain_embed, gain_in, gain_out, w_left, w_right, w_gate, w_out):
    rows, tokens, width = pair_map.shape
    n_ax = lax.axis_size("ax")
    ax, nr = lax.axis_index("ax"), lax.axis_index("nr")
    band, tile = BAND, 8
    odd, even = list(range(n_ax - 1, 0, -2)), list(range(n_ax - 2, -1, -2))
    both = 2 * rows
    window = band + 16
    vmem = pl.BlockSpec(memory_space=pltpu.VMEM)
    smem = pl.BlockSpec(memory_space=pltpu.SMEM)
    hbm = pl.BlockSpec(memory_space=pltpu.HBM)

    def swap_core(x):
        return lax.ppermute(x, "nr", [(0, 1), (1, 0)])

    def swap(x, bit):
        pairs = []
        for s in range(n_ax):
            for core in range(2):
                pairs.append((s * 2 + core, place_of(bit, s, core) * 2 + core))
        return lax.ppermute(x, ("ax", "nr"), pairs)

    def after(x, done):
        return lax.optimization_barrier((x, done))[0]

    start = band_start[0]
    own_row, other_row = (ax * 2 + nr) * rows, (ax * 2 + 1 - nr) * rows
    meta = jnp.stack([ax, nr, own_row, other_row, start, jnp.minimum(start // 16 * 16, tokens - window)]).astype(I32)

    part_shape = jax.ShapeDtypeStruct((rows, n_ax // 2, rows, width), BF16)
    weights = jnp.concatenate([w_left, w_right, w_gate.T, w_out.T], 0)
    own_first, far, near = pl.pallas_call(
        functools.partial(pack_kernel, odd, even),
        in_specs=[smem, hbm],
        out_specs=[vmem] * 3,
        out_shape=[jax.ShapeDtypeStruct((rows, window, width), BF16), part_shape, part_shape],
        scratch_shapes=[pltpu.SemaphoreType.DMA((1 + n_ax,))],
        compiler_params=pltpu.CompilerParams(vmem_limit_bytes=10 << 20),
        name="pack",
    )(meta, pair_map)
    other_weights = swap_core(weights)
    other_first = swap_core(own_first)
    other_far = swap_core(lax.optimization_barrier((far, other_first, other_weights))[0])
    own_blocks = pair_map.reshape(rows, tokens // rows, rows, width)
    chain_cols = jnp.broadcast_to(chain_ids[:, None], (tokens, 128))
    row_mask = jnp.broadcast_to(
        lax.dynamic_slice_in_dim(token_mask, own_row, rows).astype(F32)[:, None], (rows, width)
    )
    embed, gain, gain_o = chain_embed[None], gain_in[None], gain_out[None]

    right, w_left, w_gate, w_out, own_band = pl.pallas_call(
        right_kernel,
        grid_spec=pltpu.PrefetchScalarGridSpec(
            num_scalar_prefetch=3,
            grid=(),
            in_specs=[vmem] * 7,
            out_specs=[vmem] * 5,
            scratch_shapes=[
                pltpu.VMEM(((both + 1) * (window + 8), width), F32),
                pltpu.VMEM(((width + 1) * (band + 8), 2 * both), F32),
            ],
        ),
        out_shape=[
            jax.ShapeDtypeStruct((width // 2, 2 * band, 2 * both), BF16),
            jax.ShapeDtypeStruct((2 * width, width), BF16),
            jax.ShapeDtypeStruct((width, width), BF16),
            jax.ShapeDtypeStruct((width, width), BF16),
            jax.ShapeDtypeStruct((band, rows, width), BF16),
        ],
        compiler_params=pltpu.CompilerParams(vmem_limit_bytes=18 << 20),
        cost_estimate=pl.CostEstimate(flops=4 * 10**9, bytes_accessed=2 * 10**6, transcendentals=0),
        name="right",
    )(chain_ids, token_mask, meta, own_first, other_first, weights, other_weights, chain_cols, embed, gain)

    other_near = swap_core(after(near, right))

    def triangle(labels, other_part, out_type, stacks, scalars):
        group = len(labels)
        row_specs, part_specs, chain_specs = [], [], []
        for v in labels:
            row_specs.append(
                pl.BlockSpec(
                    (tile, 1, rows, width),
                    lambda t, c, m, meta, v=v: (t, place_of(v, meta[0], meta[1]) * 2 + meta[1], 0, 0),
                )
            )
            at = (odd if v & 1 else even).index(v)
            part_specs.append(pl.BlockSpec((tile, 1, rows, width), lambda t, c, m, meta, at=at: (t, at, 0, 0)))
            chain_specs.append(
                pl.BlockSpec((rows, 128), lambda t, c, m, meta, v=v: (place_of(v, meta[0], meta[1]) * 2 + meta[1], 0))
            )
        whole = lambda shape: pl.BlockSpec(shape, lambda t, c, m, meta: (0,) * len(shape))
        out_shapes = [(stack * band, rows, width) for stack in stacks]
        return pl.pallas_call(
            functools.partial(triangle_kernel, group, tile, stacks, out_type),
            grid_spec=pltpu.PrefetchScalarGridSpec(
                num_scalar_prefetch=3,
                grid=(rows // tile,),
                in_specs=row_specs
                + part_specs
                + chain_specs
                + [whole((1, width)), whole((1, width)), whole(w_left.shape), whole(right.shape)],
                out_specs=[whole(shape) for shape in out_shapes],
                scratch_shapes=[
                    pltpu.VMEM(((width + 1) * (both + 8), group * rows), F32),
                    pltpu.VMEM(((width + 1) * (band + 8), group * rows), F32),
                ],
            ),
            out_shape=[jax.ShapeDtypeStruct(shape, out_type) for shape in out_shapes],
            compiler_params=pltpu.CompilerParams(vmem_limit_bytes=28 << 20),
            cost_estimate=pl.CostEstimate(flops=8 * 10**9, bytes_accessed=4 * 10**6, transcendentals=0),
            name="triangle",
        )(
            chain_ids, token_mask, scalars, *([own_blocks] * group), *([other_part] * group), *([chain_cols] * group),
            embed, gain, w_left, right,
        )

    size = GROUP
    far_stacks, kept = [], {}

    def far_call(at, stacks, scalars):
        labels = odd[at : at + sum(stacks)]
        for x in triangle(labels, other_far, BF16, stacks, scalars):
            count = x.shape[0] // band
            far_stacks.append((labels[:count], x))
            labels = labels[count:]

    far_call(0, (2,), meta)
    last = far_stacks[-1][1]
    for at in range(0, len(even), size):
        labels = even[at : at + size]
        kept.update(zip(labels, triangle(labels, other_near, F32, (1,) * size, after(meta, last))))
        last = kept[labels[-1]]
    gate = pl.pallas_call(
        gate_kernel,
        in_specs=[vmem] * 3,
        out_specs=vmem,
        out_shape=jax.ShapeDtypeStruct((band, rows, width), F32),
        compiler_params=pltpu.CompilerParams(vmem_limit_bytes=10 << 20),
        cost_estimate=pl.CostEstimate(flops=10**9, bytes_accessed=2 * 10**6, transcendentals=0),
        name="gate",
    )(own_band, w_gate, after(row_mask, kept[0]))

    arrived = {v: [(kept[v], 0)] for v in even}

    def send_far(n, *earlier):
        labels, x = far_stacks[n]
        for y in earlier:
            x = after(x, y)
        moved = swap(x, 1)
        for m, label in enumerate(labels):
            arrived[label - 1].append((moved, m * band))
        return moved

    def total(v):
        if len(arrived[v]) > 2:
            parts, offsets = zip(*arrived[v])
            return pl.pallas_call(
                functools.partial(merge_kernel, offsets),
                in_specs=[vmem] * len(parts),
                out_specs=vmem,
                out_shape=jax.ShapeDtypeStruct((band, rows, width), BF16),
                compiler_params=pltpu.CompilerParams(vmem_limit_bytes=8 << 20),
                cost_estimate=pl.CostEstimate(flops=10**6, bytes_accessed=10**5, transcendentals=0),
                name="merge",
            )(*parts)
        return sum(piece[start : start + band].astype(F32) for piece, start in arrived[v]).astype(BF16)

    def send(v, x=None):
        x = total(v) if x is None else x
        bit = v & -v
        moved = swap(x, bit)
        arrived[v - bit].append((moved, 0))
        return moved

    send_far(0)
    x = total(even[0])
    moved = send(even[0], x)
    for at in range(2, len(odd), 2):
        far_call(at, (1, 1), after(meta, x))
        x = far_stacks[-1][1]
    for n in range(1, len(far_stacks)):
        send_far(n)
    for v in even[1:-1]:
        send(v)

    pieces, starts = zip(*arrived[0])
    return pl.pallas_call(
        functools.partial(final_kernel, starts),
        in_specs=[vmem] * (len(pieces) + 3),
        out_specs=vmem,
        out_shape=jax.ShapeDtypeStruct((rows, band, width), BF16),
        scratch_shapes=[pltpu.VMEM(((rows + 1) * (band + 8), width), F32)],
        compiler_params=pltpu.CompilerParams(vmem_limit_bytes=14 << 20),
        cost_estimate=pl.CostEstimate(flops=10**9, bytes_accessed=3 * 10**6, transcendentals=0),
        name="final",
    )(*pieces, gate, gain_o, w_out)


def solution(mesh):
    in_specs = (
        P(("grp", "ax", "nr"), None, None),
        P("grp"),
        P("grp"),
        P("grp"),
        P(),
        P(),
        P(),
        P(None, "nr"),
        P(None, "nr"),
        P(None, "nr"),
        P(None, "nr"),
    )
    out_specs = P(("grp", "ax", "nr"), None, None)
    return jax.shard_map(body, mesh=mesh, in_specs=in_specs, out_specs=out_specs, check_vma=False)
```

```python
import functools

import jax
import jax.numpy as jnp
from jax import lax
from jax.experimental import pallas as pl
from jax.experimental.pallas import tpu as pltpu
from jax.sharding import PartitionSpec as P

BAND = 48
NORM_EPS = 1e-05
GROUP = 4
F32, BF16, I32 = jnp.float32, jnp.bfloat16, jnp.int32
LAST = (((1,), (1,)), ((), ()))


def layer_norm(values, gain):
    mean = jnp.mean(values, -1, keepdims=True)
    centered = values - mean
    var = jnp.mean(centered * centered, -1, keepdims=True)
    return centered * lax.rsqrt(var + NORM_EPS) * gain


def place_of(label, ax, nr):
    swapped = (label & ~3) | ((label & 1) << 1) | ((label >> 1) & 1)
    return ax ^ (label + (swapped - label) * nr)


def pack_kernel(far_labels, near_labels, meta, pairs, first, far, near, sems):
    window = first.shape[1]
    ax, other = meta[0], 1 - meta[1]
    base = pl.multiple_of(meta[5], 16)
    copies = [pltpu.make_async_copy(pairs.at[:, pl.ds(base, window), :], first, sems.at[0])]
    size = far.shape[2]
    for part, labels in ((far, far_labels), (near, near_labels)):
        for m, label in enumerate(labels):
            block = place_of(label, ax, other) * 2 + other
            rows = pl.ds(pl.multiple_of(block * size, size), size)
            copies.append(pltpu.make_async_copy(pairs.at[:, rows, :], part.at[:, m], sems.at[len(copies)]))
    for copy in copies:
        copy.start()
    for copy in copies:
        copy.wait()


def right_kernel(
    chain_s, mask_s, meta, own, other, own_weights, other_weights, chain_cols, embed, gain, right_ref, w_left_ref, w_gate_ref, w_out_ref, band_ref,
    normed_scr, right_scr,
):
    rows, window, width = own.shape
    band = BAND
    both = 2 * rows
    pitch, turn = window + 8, band + 8
    base = pl.multiple_of(meta[5], 16)
    offset = meta[4] - meta[5]
    first = meta[1] == 0
    chains = chain_cols[pl.ds(base, window), :]
    emb, gn = embed[...], gain[...]
    half = own_weights.shape[0] // 3

    def rows_first(ref):
        turned = [ref[n * half : (n + 1) * half].astype(F32).T.astype(BF16) for n in range(2)]
        return jnp.concatenate(turned + [ref[2 * half :]], 0)

    w_own, w_other = rows_first(own_weights), rows_first(other_weights)
    low, high = jnp.where(first, w_own, w_other), jnp.where(first, w_other, w_own)

    def weight(start, size):
        return jnp.concatenate([low[start : start + size], high[start : start + size]], 0)

    w_left_ref[...] = weight(0, width)
    w_right = weight(width, width)
    w_gate_ref[...] = weight(2 * width, width // 2)
    w_out_ref[...] = weight(2 * width + width // 2, width // 2)
    for source, start, ref in ((0, meta[2], own), (1, meta[3], other)):
        for k in range(rows):
            same = chains == chain_s[start + k]
            shifted = ref[k, 0:window].astype(F32) + jnp.where(same, emb, 0.0)
            keep = mask_s[start + k].astype(F32)
            row = (source * rows + k) * pitch
            normed_scr[row : row + window, :] = layer_norm(shifted, gn * keep)
    channel = lax.broadcasted_iota(I32, (width, 2 * both), 0)
    lane = lax.broadcasted_iota(I32, (width, 2 * both), 1)
    spread = ((channel & 1) == lane // both).astype(F32)
    for j in range(0, band, 2):
        normed = [normed_scr[pl.ds(offset + j + u, both, stride=pitch), :].astype(BF16) for u in range(2)]
        doubled = jnp.concatenate([normed[0], normed[0], normed[1], normed[1]], 0)
        proj = lax.dot_general(w_right, doubled, LAST, preferred_element_type=F32)
        edge = jax.nn.sigmoid(proj[:width]) * proj[width:]
        for u in range(2):
            keep = spread * mask_s[meta[4] + j + u].astype(F32)
            right_scr[pl.ds(j + u, width, stride=turn), :] = edge[:, u * 2 * both : (u + 1) * 2 * both] * keep
            band_ref[j + u] = normed[u][0:rows]
    for g in range(width // 2):
        pair = [right_scr[(2 * g + u) * turn : (2 * g + u) * turn + band, :] for u in range(2)]
        right_ref[g] = jnp.concatenate(pair, 0).astype(BF16)


def gate_kernel(band_ref, w_gate, mask_i, gate_ref):
    band, rows, width = band_ref.shape
    gate = lax.dot_general(band_ref[...].reshape(band * rows, width), w_gate[...], LAST, preferred_element_type=F32)
    gate_ref[...] = jax.nn.sigmoid(gate).reshape(band, rows, width) * mask_i[...][None]


def triangle_kernel(group, tile, stacks, out_type, chain_s, mask_s, meta, *refs):
    own = refs[:group]
    other = refs[group : 2 * group]
    chain_cols = refs[2 * group : 3 * group]
    embed, gain, w_left_ref, right_ref = refs[3 * group : 3 * group + 4]
    outs = refs[3 * group + 4 : -2]
    slots = [(n, m) for n, stack in enumerate(stacks) for m in range(stack)]
    left_scr, tri_scr = refs[-2:]
    pairs, band2, both2 = right_ref.shape
    width, band, both = pairs * 2, band2 // 2, both2 // 2
    rows = both // 2
    pitch, turn = both + 8, band + 8
    size = own[0].shape[2]
    lanes = group * size
    step = pl.program_id(0)
    w_left = w_left_ref[...]
    chains = jnp.concatenate([ref[...] for ref in chain_cols], 0)
    emb, gn = embed[...], gain[...]

    def normed(source, k):
        base = meta[3] if source else meta[2]
        values = jnp.concatenate([ref[k, 0] for ref in (other if source else own)], 0)
        same = chains == chain_s[base + step * tile + k]
        return layer_norm(values.astype(F32) + jnp.where(same, emb, 0.0), gn).astype(BF16)

    wide = 2 * width // (2 * lanes)
    for k in range(0, tile, wide):
        several = jnp.concatenate([normed(source, k + m) for source in range(2) for m in range(wide)], 0)
        proj = lax.dot_general(w_left, several, LAST, preferred_element_type=F32)
        edge = jax.nn.sigmoid(proj[:width]) * proj[width:]
        for n in range(2 * wide):
            at = step * tile + k + n // wide * rows + n % wide
            left_scr[pl.ds(at, width, stride=pitch), :] = edge[:, n * lanes : (n + 1) * lanes]

    @pl.when(step == pl.num_programs(0) - 1)
    def _():
        for g in range(pairs):
            left = jnp.concatenate([left_scr[c * pitch : c * pitch + both, :] for c in (2 * g, 2 * g + 1)], 0)
            tri = jnp.dot(right_ref[g], left.astype(BF16), preferred_element_type=F32)
            tri_scr[2 * g * turn : 2 * g * turn + band, :] = tri[:band]
            tri_scr[(2 * g + 1) * turn : (2 * g + 1) * turn + band, :] = tri[band:]
        for j in range(band):
            turned = tri_scr[pl.ds(j, width, stride=turn), :].T
            for b in range(group):
                outs[slots[b][0]][slots[b][1] * band + j] = turned[b * size : (b + 1) * size].astype(out_type)


def merge_kernel(starts, *refs):
    out = refs[-1]
    total = refs[0][...]
    for ref, start in zip(refs[1:-1], starts[1:]):
        total = total + ref[start : start + out.shape[0]].astype(F32)
    out[...] = total.astype(BF16)


def final_kernel(starts, *refs):
    pieces = refs[: len(starts)]
    gate_ref, gain, w_out, out_ref, scr = refs[len(starts) :]
    band, rows, width = gate_ref.shape
    turn = band + 8
    total = pieces[0][...]
    for ref, start in zip(pieces[1:], starts[1:]):
        total = total + ref[start : start + band].astype(F32)
    normed = layer_norm(total.reshape(band * rows, width), gain[...]).astype(BF16)
    projected = lax.dot_general(normed, w_out[...], LAST, preferred_element_type=F32)
    for j in range(band):
        scr[pl.ds(j, rows, stride=turn), :] = projected[j * rows : (j + 1) * rows] * gate_ref[j]
    for i in range(rows):
        out_ref[i] = scr[i * turn : i * turn + band, :].astype(BF16)


def body(pair_map, chain_ids, token_mask, band_start, chain_embed, gain_in, gain_out, w_left, w_right, w_gate, w_out):
    rows, tokens, width = pair_map.shape
    n_ax = lax.axis_size("ax")
    ax, nr = lax.axis_index("ax"), lax.axis_index("nr")
    band, tile = BAND, 8
    odd, even = list(range(n_ax - 1, 0, -2)), list(range(n_ax - 2, -1, -2))
    both = 2 * rows
    window = band + 16
    vmem = pl.BlockSpec(memory_space=pltpu.VMEM)
    smem = pl.BlockSpec(memory_space=pltpu.SMEM)
    hbm = pl.BlockSpec(memory_space=pltpu.HBM)

    def swap_core(x):
        return lax.ppermute(x, "nr", [(0, 1), (1, 0)])

    def swap(x, bit):
        pairs = []
        for s in range(n_ax):
            for core in range(2):
                pairs.append((s * 2 + core, place_of(bit, s, core) * 2 + core))
        return lax.ppermute(x, ("ax", "nr"), pairs)

    def after(x, done):
        return lax.optimization_barrier((x, done))[0]

    start = band_start[0]
    own_row, other_row = (ax * 2 + nr) * rows, (ax * 2 + 1 - nr) * rows
    meta = jnp.stack([ax, nr, own_row, other_row, start, jnp.minimum(start // 16 * 16, tokens - window)]).astype(I32)

    part_shape = jax.ShapeDtypeStruct((rows, n_ax // 2, rows, width), BF16)
    weights = jnp.concatenate([w_left, w_right, w_gate.T, w_out.T], 0)
    own_first, far, near = pl.pallas_call(
        functools.partial(pack_kernel, odd, even),
        in_specs=[smem, hbm],
        out_specs=[vmem] * 3,
        out_shape=[jax.ShapeDtypeStruct((rows, window, width), BF16), part_shape, part_shape],
        scratch_shapes=[pltpu.SemaphoreType.DMA((1 + n_ax,))],
        compiler_params=pltpu.CompilerParams(vmem_limit_bytes=10 << 20),
        name="pack",
    )(meta, pair_map)
    other_weights = swap_core(weights)
    other_first = swap_core(own_first)
    other_far = swap_core(lax.optimization_barrier((far, other_first, other_weights))[0])
    own_blocks = pair_map.reshape(rows, tokens // rows, rows, width)
    chain_cols = jnp.broadcast_to(chain_ids[:, None], (tokens, 128))
    row_mask = jnp.broadcast_to(
        lax.dynamic_slice_in_dim(token_mask, own_row, rows).astype(F32)[:, None], (rows, width)
    )
    embed, gain, gain_o = chain_embed[None], gain_in[None], gain_out[None]

    right, w_left, w_gate, w_out, own_band = pl.pallas_call(
        right_kernel,
        grid_spec=pltpu.PrefetchScalarGridSpec(
            num_scalar_prefetch=3,
            grid=(),
            in_specs=[vmem] * 7,
            out_specs=[vmem] * 5,
            scratch_shapes=[
                pltpu.VMEM(((both + 1) * (window + 8), width), F32),
                pltpu.VMEM(((width + 1) * (band + 8), 2 * both), F32),
            ],
        ),
        out_shape=[
            jax.ShapeDtypeStruct((width // 2, 2 * band, 2 * both), BF16),
            jax.ShapeDtypeStruct((2 * width, width), BF16),
            jax.ShapeDtypeStruct((width, width), BF16),
            jax.ShapeDtypeStruct((width, width), BF16),
            jax.ShapeDtypeStruct((band, rows, width), BF16),
        ],
        compiler_params=pltpu.CompilerParams(vmem_limit_bytes=18 << 20),
        cost_estimate=pl.CostEstimate(flops=4 * 10**9, bytes_accessed=2 * 10**6, transcendentals=0),
        name="right",
    )(chain_ids, token_mask, meta, own_first, other_first, weights, other_weights, chain_cols, embed, gain)

    other_near = swap_core(after(near, right))

    def triangle(labels, other_part, out_type, stacks, scalars):
        group = len(labels)
        row_specs, part_specs, chain_specs = [], [], []
        for v in labels:
            row_specs.append(
                pl.BlockSpec(
                    (tile, 1, rows, width),
                    lambda t, c, m, meta, v=v: (t, place_of(v, meta[0], meta[1]) * 2 + meta[1], 0, 0),
                )
            )
            at = (odd if v & 1 else even).index(v)
            part_specs.append(pl.BlockSpec((tile, 1, rows, width), lambda t, c, m, meta, at=at: (t, at, 0, 0)))
            chain_specs.append(
                pl.BlockSpec((rows, 128), lambda t, c, m, meta, v=v: (place_of(v, meta[0], meta[1]) * 2 + meta[1], 0))
            )
        whole = lambda shape: pl.BlockSpec(shape, lambda t, c, m, meta: (0,) * len(shape))
        out_shapes = [(stack * band, rows, width) for stack in stacks]
        return pl.pallas_call(
            functools.partial(triangle_kernel, group, tile, stacks, out_type),
            grid_spec=pltpu.PrefetchScalarGridSpec(
                num_scalar_prefetch=3,
                grid=(rows // tile,),
                in_specs=row_specs
                + part_specs
                + chain_specs
                + [whole((1, width)), whole((1, width)), whole(w_left.shape), whole(right.shape)],
                out_specs=[whole(shape) for shape in out_shapes],
                scratch_shapes=[
                    pltpu.VMEM(((width + 1) * (both + 8), group * rows), F32),
                    pltpu.VMEM(((width + 1) * (band + 8), group * rows), F32),
                ],
            ),
            out_shape=[jax.ShapeDtypeStruct(shape, out_type) for shape in out_shapes],
            compiler_params=pltpu.CompilerParams(vmem_limit_bytes=28 << 20),
            cost_estimate=pl.CostEstimate(flops=8 * 10**9, bytes_accessed=4 * 10**6, transcendentals=0),
            name="triangle",
        )(
            chain_ids, token_mask, scalars, *([own_blocks] * group), *([other_part] * group), *([chain_cols] * group),
            embed, gain, w_left, right,
        )

    size = GROUP
    far_stacks, kept = [], {}

    def far_call(at, stacks, scalars):
        labels = odd[at : at + sum(stacks)]
        for x in triangle(labels, other_far, BF16, stacks, scalars):
            count = x.shape[0] // band
            far_stacks.append((labels[:count], x))
            labels = labels[count:]

    far_call(0, (2,), meta)
    last = far_stacks[-1][1]
    for at in range(0, len(even), size):
        labels = even[at : at + size]
        kept.update(zip(labels, triangle(labels, other_near, F32, (1,) * size, after(meta, last))))
        last = kept[labels[-1]]
    gate = pl.pallas_call(
        gate_kernel,
        in_specs=[vmem] * 3,
        out_specs=vmem,
        out_shape=jax.ShapeDtypeStruct((band, rows, width), F32),
        compiler_params=pltpu.CompilerParams(vmem_limit_bytes=10 << 20),
        cost_estimate=pl.CostEstimate(flops=10**9, bytes_accessed=2 * 10**6, transcendentals=0),
        name="gate",
    )(own_band, w_gate, after(row_mask, kept[0]))

    arrived = {v: [(kept[v], 0)] for v in even}

    def send_far(n, *earlier):
        labels, x = far_stacks[n]
        for y in earlier:
            x = after(x, y)
        moved = swap(x, 1)
        for m, label in enumerate(labels):
            arrived[label - 1].append((moved, m * band))
        return moved

    def total(v):
        if len(arrived[v]) > 1:
            parts, offsets = zip(*arrived[v])
            return pl.pallas_call(
                functools.partial(merge_kernel, offsets),
                in_specs=[vmem] * len(parts),
                out_specs=vmem,
                out_shape=jax.ShapeDtypeStruct((band, rows, width), BF16),
                compiler_params=pltpu.CompilerParams(vmem_limit_bytes=8 << 20),
                cost_estimate=pl.CostEstimate(flops=10**6, bytes_accessed=10**5, transcendentals=0),
                name="merge",
            )(*parts)
        return sum(piece[start : start + band].astype(F32) for piece, start in arrived[v]).astype(BF16)

    def send(v, x=None):
        x = total(v) if x is None else x
        bit = v & -v
        moved = swap(x, bit)
        arrived[v - bit].append((moved, 0))
        return moved

    send_far(0)
    x = total(even[0])
    moved = send(even[0], x)
    for at in range(2, len(odd), 2):
        far_call(at, (1, 1), after(meta, x))
        x = far_stacks[-1][1]
    for n in range(1, len(far_stacks)):
        send_far(n)
    for v in even[1:-1]:
        send(v)

    pieces, starts = zip(*arrived[0])
    return pl.pallas_call(
        functools.partial(final_kernel, starts),
        in_specs=[vmem] * (len(pieces) + 3),
        out_specs=vmem,
        out_shape=jax.ShapeDtypeStruct((rows, band, width), BF16),
        scratch_shapes=[pltpu.VMEM(((rows + 1) * (band + 8), width), F32)],
        compiler_params=pltpu.CompilerParams(vmem_limit_bytes=14 << 20),
        cost_estimate=pl.CostEstimate(flops=10**9, bytes_accessed=3 * 10**6, transcendentals=0),
        name="final",
    )(*pieces, gate, gain_o, w_out)


def solution(mesh):
    in_specs = (
        P(("grp", "ax", "nr"), None, None),
        P("grp"),
        P("grp"),
        P("grp"),
        P(),
        P(),
        P(),
        P(None, "nr"),
        P(None, "nr"),
        P(None, "nr"),
        P(None, "nr"),
    )
    out_specs = P(("grp", "ax", "nr"), None, None)
    return jax.shard_map(body, mesh=mesh, in_specs=in_specs, out_specs=out_specs, check_vma=False)
```
